512 devices in a mesh: chan: 128 (over y, z, core), period: 4 (over x).
Axes of the slice: x: 4, y: 8, z: 8, core: 2. Of those that a mesh axis runs over, the one named last changes fastest.
Arguments:
- raw_strain: bfloat16 [4, 2048, 8192], P('period', 'chan'), may hold values from -16 to 16
- bin_ids: int32 [3, 8192, 64], P(None, 'chan'), may hold values from 0 to 31, as said below
- owner_map: int32 [256], replicated, may hold values from 0 to 127, as said below
Outputs:
- stacks: float32 [512, 32, 256], P('chan')
The draws below stay inside these ranges and needn't reach their ends.
Inputs may be any that keep to these rules, and one draw needn't show every extreme that they name: `bin_ids`: for channel c of block b = c // 64 and partner block b - d, the value is l * 8 + o: the pair lies in midpoint bin 2 * (b - 1) + l with l from 0 to 3, and in offset bin o below 8. `owner_map`: nondecreasing in the bin; bin m belongs to device m // 2 or m // 2 + 1; no device owns more than 4 bins and some device owns exactly 4.
All inputs are finite; a program needn't handle non-finite values.
Results may differ from the reference program's by a relative error of at most 0.0025.
Values may be sent and summed in bfloat16 or wider, within the bound.
No kernel may reach another device: no remote copies, remote signals or barrier semaphores. Data moves between devices by JAX's collectives and lax.ppermute only.
A program may use at most 64 MiB of HBM per device.

```python
import math
import jax
import jax.numpy as jnp
from jax import lax

CH_DEV = 64
WIN = 256
NF = 128
NWIN = 8
MB_DEV = 2
NOFF = 8
NP = 32
SAMPLES = 2048
CHANNELS = 8192
PERIODS = 4
NMB = 256
CAP = 4
SLOTS = 512
N_CHAN = 128


def draw_raw_strain(key, part):
    noise_key = jax.random.fold_in(key, 11)
    gain_key = jax.random.fold_in(key, 12)
    log_gain = jax.random.uniform(gain_key, (PERIODS, 1, CHANNELS), jnp.float32, math.log(0.5), math.log(4.0))
    channel_gain = jnp.exp(log_gain)
    values = jnp.clip(jax.random.normal(noise_key, (PERIODS, SAMPLES, CHANNELS), jnp.float32), -4.0, 4.0)
    return (values * channel_gain).astype(jnp.bfloat16)


def draw_bin_ids(key, part):
    spread = max(CH_DEV // 8, 1)
    jitter = jax.random.randint(jax.random.fold_in(key, 21), (CHANNELS,), -spread, spread + 1)
    row_index = jnp.arange(CHANNELS, dtype=jnp.int32)[:, None]
    column = jnp.arange(CH_DEV, dtype=jnp.int32)[None, :]
    block_index = row_index // CH_DEV
    position = row_index + jitter[:, None]
    bin_width = CH_DEV // MB_DEV
    result = []
    for offset in range(3):
        partner = (block_index - offset) * CH_DEV + column
        partner_pos = partner + jnp.take(jitter, jnp.mod(partner, CHANNELS))
        midpoint = jnp.floor_divide(position + partner_pos, 2)
        local_bin = jnp.clip(jnp.floor_divide(midpoint, bin_width) - MB_DEV * (block_index - 1), 0, 2 * MB_DEV - 1)
        offset_bin = jnp.clip(jnp.abs(position - partner_pos) * NOFF // (3 * CH_DEV), 0, NOFF - 1)
        result.append(local_bin * NOFF + offset_bin)
    return jnp.stack(result).astype(jnp.int32)


def draw_owner_map(key, part):
    natural = NMB // MB_DEV
    moved_bins = jax.random.randint(jax.random.fold_in(key, 31), (natural,), 0, MB_DEV + 1)
    chosen = jax.random.randint(jax.random.fold_in(key, 32), (), 1, natural - 2)
    first_moved = jax.random.randint(jax.random.fold_in(key, 33), (), 0, MB_DEV)
    natural_index = jnp.arange(natural, dtype=jnp.int32)
    moved_bins = jnp.where(natural_index == chosen, MB_DEV, moved_bins)
    moved_bins = jnp.where(natural_index == chosen + 1, 0, moved_bins)
    moved_bins = jnp.where(natural_index == natural - 1, 0, moved_bins)
    moved_bins = jnp.where(natural_index == 0, first_moved, moved_bins)
    bin_index = jnp.arange(NMB, dtype=jnp.int32)
    home_owner = bin_index // MB_DEV
    shifted = (bin_index % MB_DEV >= MB_DEV - jnp.take(moved_bins, home_owner)).astype(jnp.int32)
    return (home_owner + shifted).astype(jnp.int32)


def setup_inputs(seed: int = 0) -> dict:
    key_of = jax.random.split(jax.random.key(seed), 4)
    raw_strain = draw_raw_strain(jax.random.fold_in(key_of[3], 71), 0)
    bin_ids = draw_bin_ids(jax.random.fold_in(key_of[3], 71), 0)
    owner_map = draw_owner_map(jax.random.fold_in(key_of[3], 71), 0)
    return dict(raw_strain=raw_strain, bin_ids=bin_ids, owner_map=owner_map)


def dft_table():
    sample_at = jnp.arange(WIN, dtype=jnp.int32)[:, None]
    freq_at = jnp.arange(1, NF + 1, dtype=jnp.int32)[None, :]
    phase_angle = 2.0 * math.pi / WIN * jnp.mod(sample_at * freq_at, WIN).astype(jnp.float32)
    return jnp.concatenate([jnp.cos(phase_angle), -jnp.sin(phase_angle)], axis=1).astype(jnp.bfloat16)

def lag_table():
    freq_at = jnp.arange(1, NF + 1, dtype=jnp.int32)[:, None]
    lag_at = jnp.arange(WIN, dtype=jnp.int32)[None, :]
    phase_angle = 2.0 * math.pi / WIN * jnp.mod(freq_at * lag_at, WIN).astype(jnp.float32)
    return jnp.concatenate([jnp.cos(phase_angle), -jnp.sin(phase_angle)], axis=0)

def slant_tables():
    slow_at = (jnp.arange(NP, dtype=jnp.float32) - NP // 2) / (4.0 * NP)
    offset_at = (jnp.arange(NOFF, dtype=jnp.float32) + 0.5) * (3.0 * CH_DEV / NOFF)
    freq_at = jnp.arange(1, NF + 1, dtype=jnp.float32) * (2.0 * math.pi / WIN)
    phase_angle = slow_at[:, None, None] * offset_at[None, :, None] * freq_at[None, None, :]
    return (jnp.cos(phase_angle), jnp.sin(phase_angle))

def whiten(spectra):
    power_mean = lax.optimization_barrier(jnp.mean(spectra * spectra, axis=-2, keepdims=True))
    return (spectra / jnp.sqrt(power_mean + 1e-06)).astype(jnp.bfloat16)

def slant_lags(binned):
    cos_table, sin_table = slant_tables()
    highest = lax.Precision.HIGHEST
    real_part = binned[..., :NF]
    imag_part = binned[..., NF:]
    slant_real = jnp.einsum('mof,qof->mqf', real_part, cos_table, precision=highest) + jnp.einsum('mof,qof->mqf', imag_part, sin_table, precision=highest)
    slant_imag = jnp.einsum('mof,qof->mqf', imag_part, cos_table, precision=highest) - jnp.einsum('mof,qof->mqf', real_part, sin_table, precision=highest)
    slant_spec = jnp.concatenate([slant_real, slant_imag], axis=-1)
    return jnp.einsum('mqk,kt->mqt', slant_spec, lag_table(), precision=highest)

def normalize(total_trace):
    return total_trace / jnp.sqrt(lax.optimization_barrier(jnp.mean(total_trace * total_trace, axis=-1, keepdims=True)) + 1e-06)

def period_bins(raw_period, bin_ids, dft_weights):
    windows = raw_period.reshape(NWIN, WIN, CHANNELS).astype(jnp.float32)
    spectra = jnp.einsum('wtc,tk->wkc', windows, dft_weights.astype(jnp.float32))
    whitened = whiten(spectra)
    blocks = jnp.transpose(whitened.reshape(NWIN, 2 * NF, N_CHAN, CH_DEV), (2, 0, 1, 3))
    padded = jnp.concatenate([jnp.zeros((2, NWIN, 2 * NF, CH_DEV), jnp.bfloat16), blocks], axis=0)

    def add_block(running, block_index):
        own_block = lax.dynamic_index_in_dim(padded, (block_index + 2).astype(jnp.int32), 0, keepdims=False).astype(jnp.float32)
        own_real = own_block[:, :NF, :]
        own_imag = own_block[:, NF:, :]
        for offset in range(3):
            other_block = lax.dynamic_index_in_dim(padded, (block_index + 2 - offset).astype(jnp.int32), 0, keepdims=False).astype(jnp.float32)
            other_real = other_block[:, :NF, :]
            other_imag = other_block[:, NF:, :]
            cross_real = jnp.einsum('wfi,wfj->fij', own_real, other_real) + jnp.einsum('wfi,wfj->fij', own_imag, other_imag)
            cross_imag = jnp.einsum('wfi,wfj->fij', own_imag, other_real) - jnp.einsum('wfi,wfj->fij', own_real, other_imag)
            cross_spec = jnp.concatenate([cross_real, cross_imag], axis=0).astype(jnp.bfloat16)
            cross_spec = lax.optimization_barrier(cross_spec).astype(jnp.float32)
            pair_values = cross_spec.reshape(2 * NF, CH_DEV * CH_DEV).T
            pair_ids = lax.dynamic_slice_in_dim(bin_ids[offset], (block_index * CH_DEV).astype(jnp.int32), CH_DEV, 0).reshape(-1)
            global_ids = pair_ids + MB_DEV * NOFF * (block_index - 1)
            global_ids = jnp.where(global_ids < 0, NMB * NOFF, global_ids).astype(jnp.int32)
            running = running + jax.ops.segment_sum(pair_values, global_ids, num_segments=NMB * NOFF)
        return (running, None)
    start_sum = jnp.zeros((NMB * NOFF, 2 * NF), jnp.float32)
    running, unused = lax.scan(add_block, start_sum, jnp.arange(N_CHAN, dtype=jnp.int32))
    return running.reshape(NMB, NOFF, 2 * NF)

def reference(raw_strain, bin_ids, owner_map):
    dft_weights = dft_table()
    total_trace = jnp.zeros((NMB, NP, WIN), jnp.float32)
    for period in range(PERIODS):
        binned = period_bins(raw_strain[period], bin_ids, dft_weights)
        total_trace = total_trace + slant_lags(binned)
    normed = normalize(total_trace)
    owners_below = lax.optimization_barrier(jnp.sum((owner_map[None, :] < owner_map[:, None]).astype(jnp.int32), axis=1))
    slot_rows = (owner_map * CAP + jnp.arange(NMB, dtype=jnp.int32) - owners_below).astype(jnp.int32)
    return jnp.zeros((SLOTS, NP, WIN), jnp.float32).at[slot_rows].set(normed)
```

```python
import math

import jax
import jax.numpy as jnp
import numpy as np
from jax import lax
from jax.experimental import pallas as pl
from jax.experimental.pallas import tpu as pltpu
from jax.sharding import PartitionSpec as P

CH_DEV = 64
WIN = 256
NF = 128
NWIN = 8
MB_DEV = 2
NOFF = 8
NP = 32
CAP = 4
BINS = 2 * MB_DEV * NOFF
VMEM_LIMIT = 48 * 1024 * 1024

ROW_SAMPLE = (
    16 * np.arange(16)[None, :, None] + 8 * np.arange(2)[:, None, None] + np.arange(8)[None, None, :]
).reshape(-1)


def dft_rows():
    phase = 2.0 * math.pi / WIN * np.mod(ROW_SAMPLE[:, None] * np.arange(1, NF + 1)[None, :], WIN)
    return np.concatenate([np.cos(phase), -np.sin(phase)], axis=1).astype(np.float32)


def lag_table():
    phase = 2.0 * math.pi / WIN * np.mod(np.arange(1, NF + 1)[:, None] * np.arange(WIN)[None, :], WIN)
    return np.concatenate([np.cos(phase), -np.sin(phase)], axis=0).astype(np.float32)


def slant_tables():
    slow = (np.arange(NP) - NP // 2) / (4.0 * NP)
    offset = (np.arange(NOFF) + 0.5) * (3.0 * CH_DEV / NOFF)
    freq = np.arange(1, NF + 1) * (2.0 * math.pi / WIN)
    phase = offset[:, None, None] * slow[None, :, None] * freq[None, None, :]
    return np.stack([np.cos(phase), np.sin(phase)]).astype(np.float32)


def call(kernel, out_shape, n_in, **kw):
    return pl.pallas_call(
        kernel,
        out_shape=out_shape,
        compiler_params=pltpu.CompilerParams(vmem_limit_bytes=VMEM_LIMIT),
        **kw,
    )


def pack_kernel(raw_ref, out_ref):
    low = lax.broadcasted_iota(jnp.int32, (8, 128), 1) < 64
    for tile in range(raw_ref.shape[1] // 128):
        both = raw_ref[:, 128 * tile : 128 * tile + 128].astype(jnp.float32)
        first, second = both[:8], both[8:]
        even = jnp.where(low, first, pltpu.roll(second, 64, 1))
        odd = jnp.where(low, pltpu.roll(first, 64, 1), second)
        out_ref[tile] = jnp.concatenate([even, odd], axis=0).astype(jnp.bfloat16)


def mask_kernel(ids_ref, owner_ref, masks_ref, place_ref):
    ids = jnp.concatenate([ids_ref[0], ids_ref[1], ids_ref[2]], axis=1)
    for bin_at in range(BINS):
        masks_ref[bin_at * CH_DEV : (bin_at + 1) * CH_DEV, :] = (
            (ids == bin_at).astype(jnp.float32).astype(jnp.bfloat16)
        )
    device = lax.axis_index("chan")
    owner = owner_ref[...]
    place_ref[0] = jnp.sum((owner < device).astype(jnp.int32)) - MB_DEV * (device - 1)
    place_ref[1] = jnp.sum((owner == device).astype(jnp.int32))


def spectra_kernel(series_ref, table_ref, out_ref):
    table = table_ref[...]
    for window in range(NWIN):
        turned = series_ref[window].astype(jnp.float32).T.astype(jnp.bfloat16)
        series = jnp.concatenate([turned[:CH_DEV], turned[CH_DEV:]], axis=1)
        spectra = jnp.dot(series, table, preferred_element_type=jnp.float32)
        power = jnp.mean(spectra * spectra, axis=-1, keepdims=True)
        out_ref[window] = (spectra / jnp.sqrt(power + 1e-06)).astype(jnp.bfloat16)


def bin_kernel(masks_ref, own_ref, near_ref, far_ref, wide_ref, half_ref, sums):
    def add_window(window, carry):
        own = own_ref[window]
        partners = jnp.concatenate([own, near_ref[window], far_ref[window]], axis=0)
        own = own.astype(jnp.float32)
        own_real, own_imag = own[:, :NF], own[:, NF:]
        for bin_at in range(BINS):
            picked = jnp.dot(
                masks_ref[bin_at * CH_DEV : (bin_at + 1) * CH_DEV, :],
                partners,
                preferred_element_type=jnp.float32,
            )
            picked_real, picked_imag = picked[:, :NF], picked[:, NF:]
            real = own_real * picked_real + own_imag * picked_imag
            imag = own_imag * picked_real - own_real * picked_imag
            sums[0, bin_at] += jnp.sum(real.reshape(8, 8, NF), axis=0)
            sums[1, bin_at] += jnp.sum(imag.reshape(8, 8, NF), axis=0)
        return carry

    sums[...] = jnp.zeros_like(sums)
    lax.fori_loop(0, NWIN, add_window, 0)
    binned = jnp.concatenate([jnp.sum(sums[0], axis=1), jnp.sum(sums[1], axis=1)], axis=1)
    odd = lax.rem(lax.axis_index("chan"), 2)
    half = jnp.where(odd == 1, binned[BINS // 2 :], binned[: BINS // 2])
    for place in range(8):
        wide_ref[place] = binned
        half_ref[place] = half


def stack_kernel(place_ref, wide_ref, half_ref, slant_ref, lags_ref, out_ref, held, spec):
    device = lax.axis_index("chan")
    odd = lax.rem(device, 2)
    whole = BINS // 2

    def over_periods(ref, part, rows):
        total = ref[part * 4, rows]
        for period in range(1, 4):
            total = total + ref[part * 4 + period, rows]
        return total

    own = over_periods(wide_ref, odd, pl.ds(0, BINS))
    beside = over_periods(wide_ref, 1 - odd, pl.ds(pl.multiple_of(odd * whole, 8), whole))
    across = over_periods(half_ref, 1 - odd, pl.ds(0, whole))
    has_across = (device > 0) & (device < lax.axis_size("chan") - 1)
    across = jnp.where(has_across, across, 0.0)
    lower = own[:whole] + jnp.where(odd == 1, beside, across)
    upper = own[whole:] + jnp.where(odd == 1, across, beside)
    held[...] = jnp.zeros_like(held)
    held[:whole] = lower
    held[whole:BINS] = upper
    first = place_ref[0]
    count = place_ref[1]
    first = jnp.where(count > 0, first, 0)
    for slot in range(CAP):
        rows = held[pl.ds(pl.multiple_of((first + slot) * NOFF, 8), NOFF), :]
        rows = jnp.where(slot < count, rows, 0.0)
        real = jnp.zeros((NP, NF), jnp.float32)
        imag = jnp.zeros((NP, NF), jnp.float32)
        for offset in range(NOFF):
            bin_real = rows[offset : offset + 1, :NF]
            bin_imag = rows[offset : offset + 1, NF:]
            cos, sin = slant_ref[0, offset], slant_ref[1, offset]
            real = real + (bin_real * cos + bin_imag * sin)
            imag = imag + (bin_imag * cos - bin_real * sin)
        spec[slot * NP : (slot + 1) * NP, :NF] = real
        spec[slot * NP : (slot + 1) * NP, NF:] = imag
    traces = jnp.dot(
        spec[...], lags_ref[...], precision=lax.Precision.HIGHEST, preferred_element_type=jnp.float32
    )
    power = jnp.mean(traces * traces, axis=-1, keepdims=True)
    out_ref[...] = traces / jnp.sqrt(power + 1e-06)


def shards(raw_strain, bin_ids, owner_map):
    count = lax.axis_size("chan")
    periods = lax.axis_size("period")
    smem = pl.BlockSpec(memory_space=pltpu.SMEM)
    vmem = pl.BlockSpec(memory_space=pltpu.VMEM)
    packed = call(pack_kernel, jax.ShapeDtypeStruct((count // 2, 16, 128), jnp.bfloat16), 1)(raw_strain[0])
    series = lax.all_to_all(packed.reshape(count, 8, 128), "chan", 0, 0, tiled=True)
    masks, place = call(
        mask_kernel,
        (
            jax.ShapeDtypeStruct((BINS * CH_DEV, 3 * CH_DEV), jnp.bfloat16),
            jax.ShapeDtypeStruct((2,), jnp.int32),
        ),
        2,
        out_specs=(vmem, smem),
    )(bin_ids, owner_map.reshape(2, 128))
    own = call(spectra_kernel, jax.ShapeDtypeStruct((NWIN, CH_DEV, 2 * NF), jnp.bfloat16), 2)(
        series.reshape(NWIN, 128, 128), jnp.asarray(dft_rows(), jnp.bfloat16)
    )
    near = lax.ppermute(own, "chan", [(i, i + 1) for i in range(count - 1)])
    far = lax.ppermute(own, "chan", [(i, i + 2) for i in range(count - 2)])
    wide, half = call(
        bin_kernel,
        (
            jax.ShapeDtypeStruct((8, BINS, 2 * NF), jnp.float32),
            jax.ShapeDtypeStruct((8, BINS // 2, 2 * NF), jnp.float32),
        ),
        4,
        scratch_shapes=[pltpu.VMEM((2, BINS, 8, NF), jnp.float32)],
    )(masks, own, near, far)
    chip_pairs = [(2 * k, 2 * k + 1) for k in range(count // 2)]
    cross_pairs = [((2 * k + 2) % count, 2 * k + 1) for k in range(count // 2)]
    both = ("chan", "period")
    groups = [[c * periods + p for c in pair for p in range(periods)] for pair in chip_pairs]
    wide = lax.all_to_all(wide, both, 0, 0, tiled=True, axis_index_groups=groups)
    groups = [[c * periods + p for c in pair for p in range(periods)] for pair in cross_pairs]
    half = lax.all_to_all(half, both, 0, 0, tiled=True, axis_index_groups=groups)
    stacks = call(
        stack_kernel,
        jax.ShapeDtypeStruct((CAP * NP, WIN), jnp.float32),
        5,
        in_specs=[smem, vmem, vmem, vmem, vmem],
        scratch_shapes=[pltpu.VMEM((2 * BINS, 2 * NF), jnp.float32), pltpu.VMEM((CAP * NP, 2 * NF), jnp.float32)],
    )(place, wide, half, jnp.asarray(slant_tables()), jnp.asarray(lag_table()))
    return stacks.reshape(CAP, NP, WIN)


def solution(mesh):
    placed = (P("period", "chan", None), P(None, "chan", None), P())
    return jax.shard_map(
        shards, mesh=mesh, in_specs=placed, out_specs=P("chan", None, None), check_vma=False
    )
```

```python
import math

import jax
import jax.numpy as jnp
import numpy as np
from jax import lax
from jax.experimental import pallas as pl
from jax.experimental.pallas import tpu as pltpu
from jax.sharding import PartitionSpec as P

CH_DEV = 64
WIN = 256
NF = 128
NWIN = 8
MB_DEV = 2
NOFF = 8
NP = 32
CAP = 4
BINS = 2 * MB_DEV * NOFF
VMEM_LIMIT = 48 * 1024 * 1024

ROW_SAMPLE = (
    16 * np.arange(16)[None, :, None] + 8 * np.arange(2)[:, None, None] + np.arange(8)[None, None, :]
).reshape(-1)


def dft_rows():
    phase = 2.0 * math.pi / WIN * np.mod(ROW_SAMPLE[:, None] * np.arange(1, NF + 1)[None, :], WIN)
    return np.concatenate([np.cos(phase), -np.sin(phase)], axis=1).astype(np.float32)


def lag_table():
    phase = 2.0 * math.pi / WIN * np.mod(np.arange(1, NF + 1)[:, None] * np.arange(WIN)[None, :], WIN)
    return np.concatenate([np.cos(phase), -np.sin(phase)], axis=0).astype(np.float32)


def slant_tables():
    slow = (np.arange(NP) - NP // 2) / (4.0 * NP)
    offset = (np.arange(NOFF) + 0.5) * (3.0 * CH_DEV / NOFF)
    freq = np.arange(1, NF + 1) * (2.0 * math.pi / WIN)
    phase = offset[:, None, None] * slow[None, :, None] * freq[None, None, :]
    return np.stack([np.cos(phase), np.sin(phase)]).astype(np.float32)


def call(kernel, out_shape, n_in, flops=0, **kw):
    return pl.pallas_call(
        kernel,
        out_shape=out_shape,
        cost_estimate=pl.CostEstimate(flops=flops, bytes_accessed=flops // 256, transcendentals=0),
        compiler_params=pltpu.CompilerParams(vmem_limit_bytes=VMEM_LIMIT),
        **kw,
    )


def pack_kernel(raw_ref, out_ref):
    low = lax.broadcasted_iota(jnp.int32, (8, 128), 1) < 64
    for tile in range(raw_ref.shape[1] // 128):
        both = raw_ref[:, 128 * tile : 128 * tile + 128].astype(jnp.float32)
        first, second = both[:8], both[8:]
        even = jnp.where(low, first, pltpu.roll(second, 64, 1))
        odd = jnp.where(low, pltpu.roll(first, 64, 1), second)
        out_ref[tile] = jnp.concatenate([even, odd], axis=0).astype(jnp.bfloat16)


def mask_kernel(ids_ref, masks_ref):
    ids = jnp.concatenate([ids_ref[0], ids_ref[1], ids_ref[2]], axis=1)
    for bin_at in range(BINS):
        masks_ref[bin_at * CH_DEV : (bin_at + 1) * CH_DEV, :] = (
            (ids == bin_at).astype(jnp.float32).astype(jnp.bfloat16)
        )


def place_kernel(owner_ref, place_ref):
    device = lax.axis_index("chan")
    owner = owner_ref[...]
    place_ref[0] = jnp.sum((owner < device).astype(jnp.int32)) - MB_DEV * (device - 1)
    place_ref[1] = jnp.sum((owner == device).astype(jnp.int32))


def spectra_kernel(series_ref, table_ref, out_ref):
    table = table_ref[...]
    for window in range(NWIN):
        turned = series_ref[window].astype(jnp.float32).T.astype(jnp.bfloat16)
        series = jnp.concatenate([turned[:CH_DEV], turned[CH_DEV:]], axis=1)
        spectra = jnp.dot(series, table, preferred_element_type=jnp.float32)
        power = jnp.mean(spectra * spectra, axis=-1, keepdims=True)
        out_ref[window] = (spectra / jnp.sqrt(power + 1e-06)).astype(jnp.bfloat16)


def bin_kernel(masks_ref, own_ref, near_ref, far_ref, wide_ref, half_ref, sums):
    step = 16

    def add_bins(at, carry):
        totals = None
        rows = pl.ds(pl.multiple_of(at * step * CH_DEV, step * CH_DEV), step * CH_DEV)
        for window in range(NWIN):
            own = own_ref[window]
            partners = jnp.concatenate([own, near_ref[window], far_ref[window]], axis=0)
            own = own.astype(jnp.float32)
            own_real, own_imag = own[:, :NF], own[:, NF:]
            picked = jnp.dot(masks_ref[rows, :], partners, preferred_element_type=jnp.float32)
            terms = []
            for bin_at in range(step):
                picked_real = picked[bin_at * CH_DEV : (bin_at + 1) * CH_DEV, :NF]
                picked_imag = picked[bin_at * CH_DEV : (bin_at + 1) * CH_DEV, NF:]
                real = own_real * picked_real + own_imag * picked_imag
                imag = own_imag * picked_real - own_real * picked_imag
                terms.append(jnp.sum(real.reshape(8, 8, NF), axis=0))
                terms.append(jnp.sum(imag.reshape(8, 8, NF), axis=0))
            totals = terms if totals is None else [x + y for x, y in zip(totals, terms)]
        for bin_at in range(step):
            sums[0, at * step + bin_at] = totals[2 * bin_at]
            sums[1, at * step + bin_at] = totals[2 * bin_at + 1]
        return carry

    lax.fori_loop(0, BINS // step, add_bins, 0)
    binned = jnp.concatenate([jnp.sum(sums[0], axis=1), jnp.sum(sums[1], axis=1)], axis=1)
    odd = lax.rem(lax.axis_index("chan"), 2)
    half = jnp.where(odd == 1, binned[BINS // 2 :], binned[: BINS // 2])
    for place in range(8):
        wide_ref[place] = binned.astype(jnp.bfloat16)
        half_ref[place] = half.astype(jnp.bfloat16)


def stack_kernel(place_ref, wide_ref, half_ref, slant_ref, lags_ref, out_ref, held, spec):
    device = lax.axis_index("chan")
    odd = lax.rem(device, 2)
    whole = BINS // 2

    def over_periods(ref, part, rows):
        total = ref[part * 4, rows].astype(jnp.float32)
        for period in range(1, 4):
            total = total + ref[part * 4 + period, rows].astype(jnp.float32)
        return total

    own = over_periods(wide_ref, odd, pl.ds(0, BINS))
    beside = over_periods(wide_ref, 1 - odd, pl.ds(pl.multiple_of(odd * whole, 16), whole))
    across = over_periods(half_ref, 1 - odd, pl.ds(0, whole))
    has_across = (device > 0) & (device < lax.axis_size("chan") - 1)
    across = jnp.where(has_across, across, 0.0)
    lower = own[:whole] + jnp.where(odd == 1, beside, across)
    upper = own[whole:] + jnp.where(odd == 1, across, beside)
    held[...] = jnp.zeros_like(held)
    held[:whole] = lower
    held[whole:BINS] = upper
    first = place_ref[0]
    count = place_ref[1]
    first = jnp.where(count > 0, first, 0)
    for slot in range(CAP):
        rows = held[pl.ds(pl.multiple_of((first + slot) * NOFF, 8), NOFF), :]
        rows = jnp.where(slot < count, rows, 0.0)
        real = jnp.zeros((NP, NF), jnp.float32)
        imag = jnp.zeros((NP, NF), jnp.float32)
        for offset in range(NOFF):
            bin_real = rows[offset : offset + 1, :NF]
            bin_imag = rows[offset : offset + 1, NF:]
            cos, sin = slant_ref[0, offset], slant_ref[1, offset]
            real = real + (bin_real * cos + bin_imag * sin)
            imag = imag + (bin_imag * cos - bin_real * sin)
        spec[slot * NP : (slot + 1) * NP, :NF] = real
        spec[slot * NP : (slot + 1) * NP, NF:] = imag
    traces = jnp.dot(
        spec[...], lags_ref[...], precision=lax.Precision.HIGHEST, preferred_element_type=jnp.float32
    )
    power = jnp.mean(traces * traces, axis=-1, keepdims=True)
    out_ref[...] = traces / jnp.sqrt(power + 1e-06)


def shards(raw_strain, bin_ids, owner_map):
    count = lax.axis_size("chan")
    periods = lax.axis_size("period")
    smem = pl.BlockSpec(memory_space=pltpu.SMEM)
    vmem = pl.BlockSpec(memory_space=pltpu.VMEM)
    packed = call(pack_kernel, jax.ShapeDtypeStruct((count // 2, 16, 128), jnp.bfloat16), 1)(raw_strain[0])
    series = lax.all_to_all(packed.reshape(count, 8, 128), "chan", 0, 0, tiled=True)
    masks = call(
        mask_kernel,
        jax.ShapeDtypeStruct((BINS * CH_DEV, 3 * CH_DEV), jnp.bfloat16),
        1,
        flops=4000000000,
    )(bin_ids)
    series, masks = lax.optimization_barrier((series, masks))
    own = call(spectra_kernel, jax.ShapeDtypeStruct((NWIN, CH_DEV, 2 * NF), jnp.bfloat16), 2)(
        series.reshape(NWIN, 128, 128), jnp.asarray(dft_rows(), jnp.bfloat16)
    )
    near = lax.ppermute(own, "chan", [(i, i + 1) for i in range(count - 1)])
    far = lax.ppermute(own, "chan", [(i, i + 2) for i in range(count - 2)])
    wide, half = call(
        bin_kernel,
        (
            jax.ShapeDtypeStruct((8, BINS, 2 * NF), jnp.bfloat16),
            jax.ShapeDtypeStruct((8, BINS // 2, 2 * NF), jnp.bfloat16),
        ),
        4,
        scratch_shapes=[pltpu.VMEM((2, BINS, 8, NF), jnp.float32)],
    )(masks, own, near, far)
    chip_pairs = [(2 * k, 2 * k + 1) for k in range(count // 2)]
    cross_pairs = [((2 * k + 2) % count, 2 * k + 1) for k in range(count // 2)]
    both = ("chan", "period")
    wide, half, owner_map = lax.optimization_barrier((wide, half, owner_map))
    groups = [[c * periods + p for c in pair for p in range(periods)] for pair in chip_pairs]
    wide = lax.all_to_all(wide, both, 0, 0, tiled=True, axis_index_groups=groups)
    groups = [[c * periods + p for c in pair for p in range(periods)] for pair in cross_pairs]
    half = lax.all_to_all(half, both, 0, 0, tiled=True, axis_index_groups=groups)
    place = call(
        place_kernel, jax.ShapeDtypeStruct((2,), jnp.int32), 1, flops=4000000000, out_specs=smem
    )(owner_map.reshape(2, 128))
    wide, half, place = lax.optimization_barrier((wide, half, place))
    stacks = call(
        stack_kernel,
        jax.ShapeDtypeStruct((CAP * NP, WIN), jnp.float32),
        5,
        in_specs=[smem, vmem, vmem, vmem, vmem],
        scratch_shapes=[pltpu.VMEM((2 * BINS, 2 * NF), jnp.float32), pltpu.VMEM((CAP * NP, 2 * NF), jnp.float32)],
    )(place, wide, half, jnp.asarray(slant_tables()), jnp.asarray(lag_table()))
    return stacks.reshape(CAP, NP, WIN)


def solution(mesh):
    placed = (P("period", "chan", None), P(None, "chan", None), P())
    return jax.shard_map(
        shards, mesh=mesh, in_specs=placed, out_specs=P("chan", None, None), check_vma=False
    )
```

```python
import functools
import math

import jax
import jax.numpy as jnp
import numpy as np
from jax import lax
from jax.experimental import pallas as pl
from jax.experimental.pallas import tpu as pltpu
from jax.sharding import PartitionSpec as P

CH_DEV = 64
WIN = 256
NF = 128
NWIN = 8
MB_DEV = 2
NOFF = 8
NP = 32
CAP = 4
BINS = 2 * MB_DEV * NOFF
HALF = BINS // 2
VMEM_LIMIT = 48 * 1024 * 1024

ROW_SAMPLE = (
    16 * np.arange(16)[None, :, None] + 8 * np.arange(2)[:, None, None] + np.arange(8)[None, None, :]
).reshape(-1)


def dft_rows():
    phase = 2.0 * math.pi / WIN * np.mod(ROW_SAMPLE[:, None] * np.arange(1, NF + 1)[None, :], WIN)
    return np.concatenate([np.cos(phase), -np.sin(phase)], axis=1).astype(np.float32)


def lag_table():
    phase = 2.0 * math.pi / WIN * np.mod(np.arange(1, NF + 1)[:, None] * np.arange(WIN)[None, :], WIN)
    return np.concatenate([np.cos(phase), -np.sin(phase)], axis=0).astype(np.float32)


def lag_parts():
    table = lag_table()
    high = table.astype(jnp.bfloat16)
    low = (table - high.astype(np.float32)).astype(jnp.bfloat16)
    return np.concatenate([high, high, low], axis=0)


def slant_tables():
    slow = (np.arange(NP) - NP // 2) / (4.0 * NP)
    offset = (np.arange(NOFF) + 0.5) * (3.0 * CH_DEV / NOFF)
    freq = np.arange(1, NF + 1) * (2.0 * math.pi / WIN)
    phase = offset[:, None, None] * slow[None, :, None] * freq[None, None, :]
    return np.stack([np.cos(phase), np.sin(phase)]).astype(np.float32)


def call(kernel, out_shape, flops=0, **kw):
    return pl.pallas_call(
        kernel,
        out_shape=out_shape,
        cost_estimate=pl.CostEstimate(flops=flops, bytes_accessed=flops // 256, transcendentals=0),
        compiler_params=pltpu.CompilerParams(vmem_limit_bytes=VMEM_LIMIT),
        **kw,
    )


def pack_kernel(raw_ref, out_ref):
    low = lax.broadcasted_iota(jnp.int32, (8, 128), 1) < 64
    for tile in range(raw_ref.shape[1] // 128):
        both = raw_ref[:, 128 * tile : 128 * tile + 128].astype(jnp.float32)
        first, second = both[:8], both[8:]
        even = jnp.where(low, first, pltpu.roll(second, 64, 1))
        odd = jnp.where(low, pltpu.roll(first, 64, 1), second)
        out_ref[tile] = jnp.concatenate([even, odd], axis=0).astype(jnp.bfloat16)


def mask_kernel(ids_ref, masks_ref):
    ids = jnp.concatenate([ids_ref[0], ids_ref[1], ids_ref[2]], axis=1)
    for bin_at in range(BINS):
        masks_ref[bin_at * CH_DEV : (bin_at + 1) * CH_DEV, :] = (
            (ids == bin_at).astype(jnp.float32).astype(jnp.bfloat16)
        )


def place_kernel(owner_ref, place_ref):
    device = lax.axis_index("chan")
    owner = owner_ref[...]
    place_ref[0] = jnp.sum((owner < device).astype(jnp.int32)) - MB_DEV * (device - 1)
    place_ref[1] = jnp.sum((owner == device).astype(jnp.int32))


def spectra_kernel(series_ref, table_ref, out_ref):
    table = table_ref[...]
    for window in range(NWIN):
        turned = series_ref[window].astype(jnp.float32).T.astype(jnp.bfloat16)
        series = jnp.concatenate([turned[:CH_DEV], turned[CH_DEV:]], axis=1)
        spectra = jnp.dot(series, table, preferred_element_type=jnp.float32)
        power = jnp.mean(spectra * spectra, axis=-1, keepdims=True)
        out_ref[window] = (spectra / jnp.sqrt(power + 1e-06)).astype(jnp.bfloat16)


def bin_kernel(across, masks_ref, own_ref, near_ref, far_ref, out_ref):
    odd = lax.rem(lax.axis_index("chan"), 2)
    part = odd if across else 1 - odd
    rows = pl.ds(pl.multiple_of(part * HALF * CH_DEV, HALF * CH_DEV), HALF * CH_DEV)
    totals = None
    for window in range(NWIN):
        own = own_ref[window]
        partners = jnp.concatenate([own, near_ref[window], far_ref[window]], axis=0)
        own = own.astype(jnp.float32)
        own_real, own_imag = own[:, :NF], own[:, NF:]
        picked = jnp.dot(masks_ref[rows, :], partners, preferred_element_type=jnp.float32)
        terms = []
        for bin_at in range(HALF):
            picked_real = picked[bin_at * CH_DEV : (bin_at + 1) * CH_DEV, :NF]
            picked_imag = picked[bin_at * CH_DEV : (bin_at + 1) * CH_DEV, NF:]
            real = own_real * picked_real + own_imag * picked_imag
            imag = own_imag * picked_real - own_real * picked_imag
            terms.append(jnp.sum(real.reshape(8, 8, NF), axis=0))
            terms.append(jnp.sum(imag.reshape(8, 8, NF), axis=0))
        totals = terms if totals is None else [x + y for x, y in zip(totals, terms)]
    for bin_at in range(HALF):
        out_ref[bin_at : bin_at + 1, :NF] = jnp.sum(totals[2 * bin_at], axis=0, keepdims=True)
        out_ref[bin_at : bin_at + 1, NF:] = jnp.sum(totals[2 * bin_at + 1], axis=0, keepdims=True)


def merge_kernel(across_ref, inside_ref, arrived_ref, out_ref):
    odd = lax.rem(lax.axis_index("chan"), 2)
    across = (across_ref[...] + arrived_ref[...]).astype(jnp.bfloat16)
    inside = inside_ref[...].astype(jnp.bfloat16)
    merged = jnp.concatenate(
        [jnp.where(odd == 1, inside, across), jnp.where(odd == 1, across, inside)], axis=0
    )
    for place in range(8):
        out_ref[place] = merged


def stack_kernel(place_ref, sums_ref, slant_ref, lags_ref, out_ref, held, spec):
    odd = lax.rem(lax.axis_index("chan"), 2)

    def over_periods(part, rows):
        total = sums_ref[part * 4, rows].astype(jnp.float32)
        for period in range(1, 4):
            total = total + sums_ref[part * 4 + period, rows].astype(jnp.float32)
        return total

    own = over_periods(odd, pl.ds(0, BINS))
    beside = over_periods(1 - odd, pl.ds(pl.multiple_of(odd * HALF, HALF), HALF))
    held[...] = jnp.zeros_like(held)
    held[:HALF] = own[:HALF] + jnp.where(odd == 1, beside, 0.0)
    held[HALF:BINS] = own[HALF:] + jnp.where(odd == 1, 0.0, beside)
    count = place_ref[1]
    first = jnp.where(count > 0, place_ref[0], 0)
    for slot in range(CAP):
        rows = held[pl.ds(pl.multiple_of((first + slot) * NOFF, 8), NOFF), :]
        rows = jnp.where(slot < count, rows, 0.0)
        real = jnp.zeros((NP, NF), jnp.float32)
        imag = jnp.zeros((NP, NF), jnp.float32)
        for offset in range(NOFF):
            bin_real = rows[offset : offset + 1, :NF]
            bin_imag = rows[offset : offset + 1, NF:]
            cos, sin = slant_ref[0, offset], slant_ref[1, offset]
            real = real + (bin_real * cos + bin_imag * sin)
            imag = imag + (bin_imag * cos - bin_real * sin)
        spec[slot * NP : (slot + 1) * NP, :NF] = real
        spec[slot * NP : (slot + 1) * NP, NF:] = imag
    whole = spec[...]
    high = whole.astype(jnp.bfloat16)
    low = (whole - high.astype(jnp.float32)).astype(jnp.bfloat16)
    traces = jnp.dot(
        jnp.concatenate([high, low, high], axis=1), lags_ref[...], preferred_element_type=jnp.float32
    )
    power = jnp.mean(traces * traces, axis=-1, keepdims=True)
    out_ref[...] = traces / jnp.sqrt(power + 1e-06)


def shards(raw_strain, bin_ids, owner_map):
    count = lax.axis_size("chan")
    periods = lax.axis_size("period")
    smem = pl.BlockSpec(memory_space=pltpu.SMEM)
    vmem = pl.BlockSpec(memory_space=pltpu.VMEM)
    packed = call(pack_kernel, jax.ShapeDtypeStruct((count // 2, 16, 128), jnp.bfloat16))(raw_strain[0])
    series = lax.all_to_all(packed.reshape(count, 8, 128), "chan", 0, 0, tiled=True)
    masks = call(
        mask_kernel,
        jax.ShapeDtypeStruct((BINS * CH_DEV, 3 * CH_DEV), jnp.bfloat16),
        flops=2000000000,
    )(bin_ids)
    own = call(spectra_kernel, jax.ShapeDtypeStruct((NWIN, CH_DEV, 2 * NF), jnp.bfloat16))(
        series.reshape(NWIN, 128, 128), jnp.asarray(dft_rows(), jnp.bfloat16)
    )
    near = lax.ppermute(own, "chan", [(i, i + 1) for i in range(count - 1)])
    far = lax.ppermute(own, "chan", [(i, i + 2) for i in range(count - 2)])
    place = call(place_kernel, jax.ShapeDtypeStruct((2,), jnp.int32), out_specs=smem)(
        owner_map.reshape(2, 128)
    )
    part = jax.ShapeDtypeStruct((HALF, 2 * NF), jnp.float32)
    across = call(functools.partial(bin_kernel, True), part)(masks, own, near, far)
    pairs = [(2 * k + 1, 2 * k + 2) for k in range(count // 2 - 1)]
    arrived = lax.ppermute(across, "chan", pairs + [(j, i) for i, j in pairs])
    inside = call(functools.partial(bin_kernel, False), part, flops=2000000000)(masks, own, near, far)
    merged = call(merge_kernel, jax.ShapeDtypeStruct((8, BINS, 2 * NF), jnp.bfloat16))(
        across, inside, arrived
    )
    groups = [
        [(2 * k + core) * periods + p for core in range(2) for p in range(periods)]
        for k in range(count // 2)
    ]
    sums = lax.all_to_all(
        merged, ("chan", "period"), 0, 0, tiled=True, axis_index_groups=groups
    )
    stacks = call(
        stack_kernel,
        jax.ShapeDtypeStruct((CAP * NP, WIN), jnp.float32),
        in_specs=[smem, vmem, vmem, vmem],
        scratch_shapes=[
            pltpu.VMEM((2 * BINS, 2 * NF), jnp.float32),
            pltpu.VMEM((CAP * NP, 2 * NF), jnp.float32),
        ],
    )(place, sums, jnp.asarray(slant_tables()), jnp.asarray(lag_parts()))
    return stacks.reshape(CAP, NP, WIN)


def solution(mesh):
    placed = (P("period", "chan", None), P(None, "chan", None), P())
    return jax.shard_map(
        shards, mesh=mesh, in_specs=placed, out_specs=P("chan", None, None), check_vma=False
    )
```

```python
import functools
import math

import jax
import jax.numpy as jnp
import numpy as np
from jax import lax
from jax.experimental import pallas as pl
from jax.experimental.pallas import tpu as pltpu
from jax.sharding import PartitionSpec as P

CH_DEV = 64
WIN = 256
NF = 128
NWIN = 8
HELD = NWIN // 2
MB_DEV = 2
NOFF = 8
NP = 32
CAP = 4
BINS = 2 * MB_DEV * NOFF
HALF = BINS // 2
VMEM_LIMIT = 48 * 1024 * 1024

def chip_at(place):
    row, chip, core = place // 16, place % 16 // 2, place % 2
    return 8 * (row + 4 * core) + chip


def dft_rows():
    phase = 2.0 * math.pi / WIN * np.mod(np.arange(WIN)[:, None] * np.arange(1, NF + 1)[None, :], WIN)
    return np.concatenate([np.cos(phase), -np.sin(phase)], axis=1).astype(np.float32)


def lag_table():
    phase = 2.0 * math.pi / WIN * np.mod(np.arange(1, NF + 1)[:, None] * np.arange(WIN)[None, :], WIN)
    return np.concatenate([np.cos(phase), -np.sin(phase)], axis=0).astype(np.float32)


def lag_parts():
    table = lag_table()
    high = table.astype(jnp.bfloat16)
    low = (table - high.astype(np.float32)).astype(jnp.bfloat16)
    return np.concatenate([high, high, low], axis=0)


def slant_tables():
    slow = (np.arange(NP) - NP // 2) / (4.0 * NP)
    offset = (np.arange(NOFF) + 0.5) * (3.0 * CH_DEV / NOFF)
    freq = np.arange(1, NF + 1) * (2.0 * math.pi / WIN)
    phase = offset[:, None, None] * slow[None, :, None] * freq[None, None, :]
    return np.stack([np.cos(phase), np.sin(phase)]).astype(np.float32)


def call(kernel, out_shape, flops=0, **kw):
    return pl.pallas_call(
        kernel,
        out_shape=out_shape,
        cost_estimate=pl.CostEstimate(flops=flops, bytes_accessed=flops // 256, transcendentals=0),
        compiler_params=pltpu.CompilerParams(vmem_limit_bytes=VMEM_LIMIT),
        **kw,
    )


def pack_kernel(raw_ref, out_ref):
    for place in range(raw_ref.shape[1] // 128):
        chip = chip_at(place)
        for tile in range(2):
            at = 128 * (chip - 1 + tile)
            if at < 0:
                out_ref[place, tile] = jnp.zeros((16, 128), jnp.bfloat16)
            else:
                out_ref[place, tile] = raw_ref[:, at : at + 128]


def mask_kernel(first_ref, second_ref, masks_ref):
    swapped = lax.axis_index("chan") >= lax.axis_size("chan") // 2
    firsts = jnp.concatenate([first_ref[2], first_ref[1], first_ref[0]], axis=1)
    seconds = jnp.concatenate([second_ref[2], second_ref[1], second_ref[0]], axis=1)
    for block in range(2):
        ids = jnp.where(swapped, firsts, seconds) if block else jnp.where(swapped, seconds, firsts)
        for bin_at in range(BINS):
            masks_ref[block, bin_at * CH_DEV : (bin_at + 1) * CH_DEV, :] = (
                (ids == bin_at).astype(jnp.float32).astype(jnp.bfloat16)
            )


def place_kernel(owner_ref, place_ref):
    device = lax.axis_index("chan")
    owner = owner_ref[...]
    place_ref[0] = jnp.sum((owner < device).astype(jnp.int32)) - MB_DEV * (device - 1)
    place_ref[1] = jnp.sum((owner == device).astype(jnp.int32))


def spectra_kernel(series_ref, table_ref, out_ref):
    table = table_ref[...]
    for window in range(HELD):
        for tile in range(2):
            series = series_ref[window, :, tile].reshape(WIN, 128).T
            spectra = jnp.dot(series, table, preferred_element_type=jnp.float32)
            power = jnp.mean(spectra * spectra, axis=-1, keepdims=True)
            out_ref[window, 128 * tile : 128 * tile + 128] = (
                spectra / jnp.sqrt(power + 1e-06)
            ).astype(jnp.bfloat16)


def bin_kernel(masks_ref, spectra_ref, whole_ref, lower_ref, upper_ref):
    def add_bins(sources):
        totals = None
        for block, half in sources:
            rows = slice(half * HALF * CH_DEV, (half + 1) * HALF * CH_DEV)
            for window in range(HELD):
                partners = spectra_ref[window, block * CH_DEV : (block + 3) * CH_DEV]
                own = spectra_ref[window, (block + 2) * CH_DEV : (block + 3) * CH_DEV]
                own = own.astype(jnp.float32)
                own_real, own_imag = own[:, :NF], own[:, NF:]
                picked = jnp.dot(
                    masks_ref[block, rows, :], partners, preferred_element_type=jnp.float32
                )
                terms = []
                for bin_at in range(HALF):
                    picked_real = picked[bin_at * CH_DEV : (bin_at + 1) * CH_DEV, :NF]
                    picked_imag = picked[bin_at * CH_DEV : (bin_at + 1) * CH_DEV, NF:]
                    real = own_real * picked_real + own_imag * picked_imag
                    imag = own_imag * picked_real - own_real * picked_imag
                    terms.append(jnp.sum(real.reshape(8, 8, NF), axis=0))
                    terms.append(jnp.sum(imag.reshape(8, 8, NF), axis=0))
                totals = terms if totals is None else [x + y for x, y in zip(totals, terms)]
        return [jnp.sum(total, axis=0, keepdims=True) for total in totals]

    for at, sources in enumerate((((0, 0),), ((0, 1), (1, 0)), ((1, 1),))):
        totals = add_bins(sources)
        for bin_at in range(HALF):
            row = jnp.concatenate(totals[2 * bin_at : 2 * bin_at + 2], axis=1)
            whole_ref[at * HALF + bin_at : at * HALF + bin_at + 1] = row
            if at == 0:
                lower_ref[bin_at : bin_at + 1] = row
            if at == 2:
                upper_ref[bin_at : bin_at + 1] = row


def merge_kernel(whole_ref, below_ref, above_ref, out_ref):
    lower = (whole_ref[:HALF] + below_ref[...]).astype(jnp.bfloat16)
    middle = whole_ref[HALF : 2 * HALF].astype(jnp.bfloat16)
    upper = (whole_ref[2 * HALF :] + above_ref[...]).astype(jnp.bfloat16)
    for period in range(4):
        out_ref[period, :HALF] = lower
        out_ref[period, HALF:] = middle
        out_ref[4 + period, :HALF] = middle
        out_ref[4 + period, HALF:] = upper


def stack_kernel(place_ref, sums_ref, slant_ref, lags_ref, out_ref, held, spec):
    total = sums_ref[0].astype(jnp.float32)
    for part in range(1, 8):
        total = total + sums_ref[part].astype(jnp.float32)
    held[...] = jnp.zeros_like(held)
    held[:BINS] = total
    count = place_ref[1]
    first = jnp.where(count > 0, place_ref[0], 0)
    for slot in range(CAP):
        rows = held[pl.ds(pl.multiple_of((first + slot) * NOFF, 8), NOFF), :]
        rows = jnp.where(slot < count, rows, 0.0)
        real = jnp.zeros((NP, NF), jnp.float32)
        imag = jnp.zeros((NP, NF), jnp.float32)
        for offset in range(NOFF):
            bin_real = rows[offset : offset + 1, :NF]
            bin_imag = rows[offset : offset + 1, NF:]
            cos, sin = slant_ref[0, offset], slant_ref[1, offset]
            real = real + (bin_real * cos + bin_imag * sin)
            imag = imag + (bin_imag * cos - bin_real * sin)
        spec[slot * NP : (slot + 1) * NP, :NF] = real
        spec[slot * NP : (slot + 1) * NP, NF:] = imag
    whole = spec[...]
    high = whole.astype(jnp.bfloat16)
    low = (whole - high.astype(jnp.float32)).astype(jnp.bfloat16)
    traces = jnp.dot(
        jnp.concatenate([high, low, high], axis=1), lags_ref[...], preferred_element_type=jnp.float32
    )
    power = jnp.mean(traces * traces, axis=-1, keepdims=True)
    out_ref[...] = traces / jnp.sqrt(power + 1e-06)


def shards(raw_strain, bin_ids, owner_map):
    count = lax.axis_size("chan")
    periods = lax.axis_size("period")
    chips = count // 2
    smem = pl.BlockSpec(memory_space=pltpu.SMEM)
    vmem = pl.BlockSpec(memory_space=pltpu.VMEM)
    holders = [(chips * part + place, chip_at(place), part) for part in range(2) for place in range(chips)]

    packed = call(pack_kernel, jax.ShapeDtypeStruct((chips, 2, 16, 128), jnp.bfloat16))(raw_strain[0])
    packed, bin_ids, owner_map = lax.optimization_barrier((packed, bin_ids, owner_map))
    groups = [list(range(chips * part, chips * (part + 1))) for part in range(2)]
    series = lax.all_to_all(packed, "chan", 0, 0, tiled=True, axis_index_groups=groups)
    first = lax.ppermute(bin_ids, "chan", [(2 * chip + part, at) for at, chip, part in holders])
    second = lax.ppermute(bin_ids, "chan", [(2 * chip + 1 - part, at) for at, chip, part in holders])
    masks = call(
        mask_kernel,
        jax.ShapeDtypeStruct((2, BINS * CH_DEV, 3 * CH_DEV), jnp.bfloat16),
        flops=2000000000,
    )(first, second)
    place = call(place_kernel, jax.ShapeDtypeStruct((2,), jnp.int32), out_specs=smem)(
        owner_map.reshape(2, 128)
    )
    series, masks, place = lax.optimization_barrier((series, masks, place))
    spectra = call(spectra_kernel, jax.ShapeDtypeStruct((HELD, 4 * CH_DEV, 2 * NF), jnp.bfloat16))(
        series.reshape(HELD, 16, 2, 16, 128), jnp.asarray(dft_rows(), jnp.bfloat16)
    )
    whole, lower, upper = call(
        bin_kernel,
        (
            jax.ShapeDtypeStruct((3 * HALF, 2 * NF), jnp.float32),
            jax.ShapeDtypeStruct((HALF, 2 * NF), jnp.float32),
            jax.ShapeDtypeStruct((HALF, 2 * NF), jnp.float32),
        ),
    )(masks, spectra)
    whole = lax.ppermute(whole, "chan", [(at, 2 * chip + part) for at, chip, part in holders])
    above = lax.ppermute(
        lower, "chan", [(at, 2 * chip - 2 + part) for at, chip, part in holders if chip > 0]
    )
    below = lax.ppermute(
        upper, "chan", [(at, 2 * chip + 2 + part) for at, chip, part in holders if chip < chips - 1]
    )
    merged = call(merge_kernel, jax.ShapeDtypeStruct((8, BINS, 2 * NF), jnp.bfloat16))(
        whole, below, above
    )
    groups = [
        [(2 * chip + core) * periods + p for core in range(2) for p in range(periods)]
        for chip in range(chips)
    ]
    sums = lax.all_to_all(
        merged, ("chan", "period"), 0, 0, tiled=True, axis_index_groups=groups
    )
    stacks = call(
        stack_kernel,
        jax.ShapeDtypeStruct((CAP * NP, WIN), jnp.float32),
        in_specs=[smem, vmem, vmem, vmem],
        scratch_shapes=[
            pltpu.VMEM((2 * BINS, 2 * NF), jnp.float32),
            pltpu.VMEM((CAP * NP, 2 * NF), jnp.float32),
        ],
    )(place, sums, jnp.asarray(slant_tables()), jnp.asarray(lag_parts()))
    return stacks.reshape(CAP, NP, WIN)


def solution(mesh):
    placed = (P("period", "chan", None), P(None, "chan", None), P())
    return jax.shard_map(
        shards, mesh=mesh, in_specs=placed, out_specs=P("chan", None, None), check_vma=False
    )
```

```python
import functools
import math

import jax
import jax.numpy as jnp
import numpy as np
from jax import lax
from jax.experimental import pallas as pl
from jax.experimental.pallas import tpu as pltpu
from jax.sharding import PartitionSpec as P

CH_DEV = 64
WIN = 256
NF = 128
NWIN = 8
PART = NWIN // 2
MB_DEV = 2
NOFF = 8
NP = 32
CAP = 4
BINS = 2 * MB_DEV * NOFF
HALF = BINS // 2
VMEM_LIMIT = 48 * 1024 * 1024

ROW_SAMPLE = (
    16 * np.arange(16)[None, :, None] + 8 * np.arange(2)[:, None, None] + np.arange(8)[None, None, :]
).reshape(-1)


def dft_rows():
    phase = 2.0 * math.pi / WIN * np.mod(ROW_SAMPLE[:, None] * np.arange(1, NF + 1)[None, :], WIN)
    return np.concatenate([np.cos(phase), -np.sin(phase)], axis=1).astype(np.float32)


def lag_table():
    phase = 2.0 * math.pi / WIN * np.mod(np.arange(1, NF + 1)[:, None] * np.arange(WIN)[None, :], WIN)
    return np.concatenate([np.cos(phase), -np.sin(phase)], axis=0).astype(np.float32)


def lag_parts():
    table = lag_table()
    high = table.astype(jnp.bfloat16)
    low = (table - high.astype(np.float32)).astype(jnp.bfloat16)
    return np.concatenate([high, high, low], axis=0)


def slant_tables():
    slow = (np.arange(NP) - NP // 2) / (4.0 * NP)
    offset = (np.arange(NOFF) + 0.5) * (3.0 * CH_DEV / NOFF)
    freq = np.arange(1, NF + 1) * (2.0 * math.pi / WIN)
    phase = offset[:, None, None] * slow[None, :, None] * freq[None, None, :]
    return np.stack([np.cos(phase), np.sin(phase)]).astype(np.float32)


def call(kernel, out_shape, flops=0, **kw):
    return pl.pallas_call(
        kernel,
        out_shape=out_shape,
        cost_estimate=pl.CostEstimate(flops=flops, bytes_accessed=flops // 256, transcendentals=0),
        compiler_params=pltpu.CompilerParams(vmem_limit_bytes=VMEM_LIMIT),
        **kw,
    )


def pack_kernel(raw_ref, out_ref):
    low = lax.broadcasted_iota(jnp.int32, (8, 128), 1) < 64
    for tile in range(raw_ref.shape[1] // 128):
        both = raw_ref[:, 128 * tile : 128 * tile + 128].astype(jnp.float32)
        first, second = both[:8], both[8:]
        even = jnp.where(low, first, pltpu.roll(second, 64, 1))
        odd = jnp.where(low, pltpu.roll(first, 64, 1), second)
        out_ref[tile] = jnp.concatenate([even, odd], axis=0).astype(jnp.bfloat16)


def mask_kernel(ids_ref, owner_ref, masks_ref, place_ref):
    ids = jnp.concatenate([ids_ref[0], ids_ref[1], ids_ref[2]], axis=1)
    for bin_at in range(BINS):
        masks_ref[bin_at * CH_DEV : (bin_at + 1) * CH_DEV, :] = (
            (ids == bin_at).astype(jnp.float32).astype(jnp.bfloat16)
        )
    device = lax.axis_index("chan")
    owner = owner_ref[...]
    place_ref[0] = jnp.sum((owner < device).astype(jnp.int32)) - MB_DEV * (device - 1)
    place_ref[1] = jnp.sum((owner == device).astype(jnp.int32))


def spectra_kernel(series_ref, table_ref, out_ref, *part_refs):
    table = table_ref[...]
    for window in range(NWIN):
        turned = series_ref[window].T
        series = jnp.concatenate([turned[:CH_DEV], turned[CH_DEV:]], axis=1)
        spectra = jnp.dot(series, table, preferred_element_type=jnp.float32)
        power = jnp.mean(spectra * spectra, axis=-1, keepdims=True)
        whitened = (spectra / jnp.sqrt(power + 1e-06)).astype(jnp.bfloat16)
        out_ref[window] = whitened
        part_refs[window // PART][window % PART] = whitened


def bin_half(masks_ref, rows, own_ref, near_ref, start, relay_ref, far_ref):
    odd = lax.rem(lax.axis_index("chan"), 2)
    totals = None
    for window in range(PART):
        own = own_ref[start + window]
        near = jnp.where(odd == 1, near_ref[start + window], relay_ref[window])
        partners = jnp.concatenate([own, near, far_ref[window]], axis=0)
        own = own.astype(jnp.float32)
        own_real, own_imag = own[:, :NF], own[:, NF:]
        picked = jnp.dot(masks_ref[rows, :], partners, preferred_element_type=jnp.float32)
        terms = []
        for bin_at in range(HALF):
            picked_real = picked[bin_at * CH_DEV : (bin_at + 1) * CH_DEV, :NF]
            picked_imag = picked[bin_at * CH_DEV : (bin_at + 1) * CH_DEV, NF:]
            real = own_real * picked_real + own_imag * picked_imag
            imag = own_imag * picked_real - own_real * picked_imag
            terms.append(jnp.sum(real.reshape(8, 8, NF), axis=0))
            terms.append(jnp.sum(imag.reshape(8, 8, NF), axis=0))
        totals = terms if totals is None else [x + y for x, y in zip(totals, terms)]
    sums = [jnp.sum(total, axis=0, keepdims=True) for total in totals]
    return [jnp.concatenate(sums[2 * k : 2 * k + 2], axis=1) for k in range(HALF)]


def first_kernel(masks_ref, own_ref, near_ref, relay_ref, far_ref, out_ref):
    for half in range(2):
        rows = pl.ds(half * HALF * CH_DEV, HALF * CH_DEV)
        for bin_at, row in enumerate(bin_half(masks_ref, rows, own_ref, near_ref, 0, relay_ref, far_ref)):
            out_ref[half, bin_at : bin_at + 1] = row


def second_kernel(across, masks_ref, sums_ref, own_ref, near_ref, relay_ref, far_ref, out_ref):
    odd = lax.rem(lax.axis_index("chan"), 2)
    half = odd if across else 1 - odd
    rows = pl.ds(pl.multiple_of(half * HALF * CH_DEV, HALF * CH_DEV), HALF * CH_DEV)
    sums = bin_half(masks_ref, rows, own_ref, near_ref, PART, relay_ref, far_ref)
    for bin_at, row in enumerate(sums):
        out_ref[bin_at : bin_at + 1] = sums_ref[half, bin_at : bin_at + 1] + row


def merge_kernel(across_ref, inside_ref, arrived_ref, out_ref):
    odd = lax.rem(lax.axis_index("chan"), 2)
    across = (across_ref[...] + arrived_ref[...]).astype(jnp.bfloat16)
    inside = inside_ref[...].astype(jnp.bfloat16)
    merged = jnp.concatenate(
        [jnp.where(odd == 1, inside, across), jnp.where(odd == 1, across, inside)], axis=0
    )
    for place in range(8):
        out_ref[place] = merged


def stack_kernel(place_ref, sums_ref, slant_ref, lags_ref, out_ref, held, spec):
    odd = lax.rem(lax.axis_index("chan"), 2)

    def over_periods(part, rows):
        total = sums_ref[part * 4, rows].astype(jnp.float32)
        for period in range(1, 4):
            total = total + sums_ref[part * 4 + period, rows].astype(jnp.float32)
        return total

    own = over_periods(odd, pl.ds(0, BINS))
    beside = over_periods(1 - odd, pl.ds(pl.multiple_of(odd * HALF, HALF), HALF))
    held[...] = jnp.zeros_like(held)
    held[:HALF] = own[:HALF] + jnp.where(odd == 1, beside, 0.0)
    held[HALF:BINS] = own[HALF:] + jnp.where(odd == 1, 0.0, beside)
    count = place_ref[1]
    first = jnp.where(count > 0, place_ref[0], 0)
    for slot in range(CAP):
        rows = held[pl.ds(pl.multiple_of((first + slot) * NOFF, 8), NOFF), :]
        rows = jnp.where(slot < count, rows, 0.0)
        real = jnp.zeros((NP, NF), jnp.float32)
        imag = jnp.zeros((NP, NF), jnp.float32)
        for offset in range(NOFF):
            bin_real = rows[offset : offset + 1, :NF]
            bin_imag = rows[offset : offset + 1, NF:]
            cos, sin = slant_ref[0, offset], slant_ref[1, offset]
            real = real + (bin_real * cos + bin_imag * sin)
            imag = imag + (bin_imag * cos - bin_real * sin)
        spec[slot * NP : (slot + 1) * NP, :NF] = real
        spec[slot * NP : (slot + 1) * NP, NF:] = imag
    whole = spec[...]
    high = whole.astype(jnp.bfloat16)
    low = (whole - high.astype(jnp.float32)).astype(jnp.bfloat16)
    traces = jnp.dot(
        jnp.concatenate([high, low, high], axis=1), lags_ref[...], preferred_element_type=jnp.float32
    )
    power = jnp.mean(traces * traces, axis=-1, keepdims=True)
    out_ref[...] = traces / jnp.sqrt(power + 1e-06)


def shards(raw_strain, bin_ids, owner_map):
    count = lax.axis_size("chan")
    periods = lax.axis_size("period")
    smem = pl.BlockSpec(memory_space=pltpu.SMEM)
    vmem = pl.BlockSpec(memory_space=pltpu.VMEM)
    packed = call(pack_kernel, jax.ShapeDtypeStruct((count // 2, 16, 128), jnp.bfloat16))(raw_strain[0])
    series = lax.all_to_all(packed.reshape(count, 8, 128), "chan", 0, 0, tiled=True)
    masks, place = call(
        mask_kernel,
        (
            jax.ShapeDtypeStruct((BINS * CH_DEV, 3 * CH_DEV), jnp.bfloat16),
            jax.ShapeDtypeStruct((2,), jnp.int32),
        ),
        flops=2000000000,
        out_specs=(vmem, smem),
    )(bin_ids, owner_map.reshape(2, 128))
    windows = jax.ShapeDtypeStruct((PART, CH_DEV, 2 * NF), jnp.bfloat16)
    whole = jax.ShapeDtypeStruct((NWIN, CH_DEV, 2 * NF), jnp.bfloat16)
    own, early, late = call(spectra_kernel, (whole, windows, windows))(
        series.reshape(NWIN, 128, 128), jnp.asarray(dft_rows(), jnp.bfloat16)
    )
    up = [(i, i + 2) for i in range(count - 2)]
    far = [lax.ppermute(part, "chan", up) for part in (early, late)]
    near = lax.ppermute(own, "chan", [(i, i + 1) for i in range(0, count, 2)])
    relay = [lax.ppermute(part, "chan", [(i + 1, i) for i in range(0, count, 2)]) for part in far]
    part = jax.ShapeDtypeStruct((HALF, 2 * NF), jnp.float32)
    first = call(
        first_kernel, jax.ShapeDtypeStruct((2, HALF, 2 * NF), jnp.float32), flops=2000000000
    )(masks, own, near, relay[0], far[0])
    second = (masks, first, own, near, relay[1], far[1])
    across = call(functools.partial(second_kernel, True), part)(*second)
    pairs = [(2 * k + 1, 2 * k + 2) for k in range(count // 2 - 1)]
    arrived = lax.ppermute(across, "chan", pairs + [(j, i) for i, j in pairs])
    inside = call(functools.partial(second_kernel, False), part, flops=1000000000)(*second)
    merged = call(merge_kernel, jax.ShapeDtypeStruct((8, BINS, 2 * NF), jnp.bfloat16))(
        across, inside, arrived
    )
    groups = [
        [(2 * k + core) * periods + p for core in range(2) for p in range(periods)]
        for k in range(count // 2)
    ]
    sums = lax.all_to_all(
        merged, ("chan", "period"), 0, 0, tiled=True, axis_index_groups=groups
    )
    stacks = call(
        stack_kernel,
        jax.ShapeDtypeStruct((CAP * NP, WIN), jnp.float32),
        in_specs=[smem, vmem, vmem, vmem],
        scratch_shapes=[
            pltpu.VMEM((2 * BINS, 2 * NF), jnp.float32),
            pltpu.VMEM((CAP * NP, 2 * NF), jnp.float32),
        ],
    )(place, sums, jnp.asarray(slant_tables()), jnp.asarray(lag_parts()))
    return stacks.reshape(CAP, NP, WIN)


def solution(mesh):
    placed = (P("period", "chan", None), P(None, "chan", None), P())
    return jax.shard_map(
        shards, mesh=mesh, in_specs=placed, out_specs=P("chan", None, None), check_vma=False
    )
```

```python
import functools
import math

import jax
import jax.numpy as jnp
import numpy as np
from jax import lax
from jax.experimental import pallas as pl
from jax.experimental.pallas import tpu as pltpu
from jax.sharding import PartitionSpec as P

CH_DEV = 64
WIN = 256
NF = 128
NWIN = 8
MB_DEV = 2
NOFF = 8
NP = 32
CAP = 4
BINS = 2 * MB_DEV * NOFF
HALF = BINS // 2
VMEM_LIMIT = 48 * 1024 * 1024

ROW_SAMPLE = (
    16 * np.arange(16)[None, :, None] + 8 * np.arange(2)[:, None, None] + np.arange(8)[None, None, :]
).reshape(-1)


def dft_rows():
    phase = 2.0 * math.pi / WIN * np.mod(ROW_SAMPLE[:, None] * np.arange(1, NF + 1)[None, :], WIN)
    return np.concatenate([np.cos(phase), -np.sin(phase)], axis=1).astype(np.float32)


def lag_table():
    phase = 2.0 * math.pi / WIN * np.mod(np.arange(1, NF + 1)[:, None] * np.arange(WIN)[None, :], WIN)
    return np.concatenate([np.cos(phase), -np.sin(phase)], axis=0).astype(np.float32)


def lag_parts():
    table = lag_table()
    high = table.astype(jnp.bfloat16)
    low = (table - high.astype(np.float32)).astype(jnp.bfloat16)
    return np.concatenate([high, high, low], axis=0)


def slant_tables():
    slow = (np.arange(NP) - NP // 2) / (4.0 * NP)
    offset = (np.arange(NOFF) + 0.5) * (3.0 * CH_DEV / NOFF)
    freq = np.arange(1, NF + 1) * (2.0 * math.pi / WIN)
    phase = offset[:, None, None] * slow[None, :, None] * freq[None, None, :]
    return np.stack([np.cos(phase), np.sin(phase)]).astype(np.float32)


def call(kernel, out_shape, flops=0, **kw):
    return pl.pallas_call(
        kernel,
        out_shape=out_shape,
        cost_estimate=pl.CostEstimate(flops=flops, bytes_accessed=flops // 256, transcendentals=0),
        compiler_params=pltpu.CompilerParams(vmem_limit_bytes=VMEM_LIMIT),
        **kw,
    )


def pack_kernel(raw_ref, out_ref):
    low = lax.broadcasted_iota(jnp.int32, (8, 128), 1) < 64
    for tile in range(raw_ref.shape[1] // 128):
        both = raw_ref[:, 128 * tile : 128 * tile + 128].astype(jnp.float32)
        first, second = both[:8], both[8:]
        even = jnp.where(low, first, pltpu.roll(second, 64, 1))
        odd = jnp.where(low, pltpu.roll(first, 64, 1), second)
        out_ref[tile] = jnp.concatenate([even, odd], axis=0).astype(jnp.bfloat16)


def mask_kernel(ids_ref, owner_ref, masks_ref, place_ref):
    ids = jnp.concatenate([ids_ref[0], ids_ref[1], ids_ref[2]], axis=1)
    for bin_at in range(BINS):
        masks_ref[bin_at * CH_DEV : (bin_at + 1) * CH_DEV, :] = (
            (ids == bin_at).astype(jnp.float32).astype(jnp.bfloat16)
        )
    device = lax.axis_index("chan")
    owner = owner_ref[...]
    place_ref[0] = jnp.sum((owner < device).astype(jnp.int32)) - MB_DEV * (device - 1)
    place_ref[1] = jnp.sum((owner == device).astype(jnp.int32))


def spectra_kernel(series_ref, table_ref, out_ref):
    table = table_ref[...]
    for window in range(NWIN):
        turned = series_ref[window].T
        series = jnp.concatenate([turned[:CH_DEV], turned[CH_DEV:]], axis=1)
        spectra = jnp.dot(series, table, preferred_element_type=jnp.float32)
        power = jnp.mean(spectra * spectra, axis=-1, keepdims=True)
        out_ref[window] = (spectra / jnp.sqrt(power + 1e-06)).astype(jnp.bfloat16)


def bin_kernel(across, masks_ref, own_ref, near_ref, far_ref, out_ref):
    odd = lax.rem(lax.axis_index("chan"), 2)
    part = odd if across else 1 - odd
    rows = pl.ds(pl.multiple_of(part * HALF * CH_DEV, HALF * CH_DEV), HALF * CH_DEV)
    totals = None
    for window in range(NWIN):
        own = own_ref[window]
        partners = jnp.concatenate([own, near_ref[window], far_ref[window]], axis=0)
        own = own.astype(jnp.float32)
        own_real, own_imag = own[:, :NF], own[:, NF:]
        picked = jnp.dot(masks_ref[rows, :], partners, preferred_element_type=jnp.float32)
        terms = []
        for bin_at in range(HALF):
            picked_real = picked[bin_at * CH_DEV : (bin_at + 1) * CH_DEV, :NF]
            picked_imag = picked[bin_at * CH_DEV : (bin_at + 1) * CH_DEV, NF:]
            real = own_real * picked_real + own_imag * picked_imag
            imag = own_imag * picked_real - own_real * picked_imag
            terms.append(jnp.sum(real.reshape(8, 8, NF), axis=0))
            terms.append(jnp.sum(imag.reshape(8, 8, NF), axis=0))
        totals = terms if totals is None else [x + y for x, y in zip(totals, terms)]
    for bin_at in range(HALF):
        out_ref[bin_at : bin_at + 1, :NF] = jnp.sum(totals[2 * bin_at], axis=0, keepdims=True)
        out_ref[bin_at : bin_at + 1, NF:] = jnp.sum(totals[2 * bin_at + 1], axis=0, keepdims=True)


def merge_kernel(across_ref, inside_ref, arrived_ref, out_ref):
    odd = lax.rem(lax.axis_index("chan"), 2)
    across = across_ref[...].astype(jnp.bfloat16)
    inside = (inside_ref[...] + arrived_ref[...]).astype(jnp.bfloat16)
    merged = jnp.concatenate(
        [jnp.where(odd == 1, inside, across), jnp.where(odd == 1, across, inside)], axis=0
    )
    for place in range(8):
        out_ref[place] = merged


def stack_kernel(place_ref, sums_ref, slant_ref, lags_ref, out_ref, held, spec):
    odd = lax.rem(lax.axis_index("chan"), 2)

    def over_periods(part, rows):
        total = sums_ref[part * 4, rows].astype(jnp.float32)
        for period in range(1, 4):
            total = total + sums_ref[part * 4 + period, rows].astype(jnp.float32)
        return total

    device = lax.axis_index("chan")
    own = over_periods(1 - odd, pl.ds(0, BINS))
    beside = over_periods(odd, pl.ds(pl.multiple_of((1 - odd) * HALF, HALF), HALF))
    beside = jnp.where((device > 0) & (device < lax.axis_size("chan") - 1), beside, 0.0)
    held[...] = jnp.zeros_like(held)
    held[:HALF] = own[:HALF] + jnp.where(odd == 1, 0.0, beside)
    held[HALF:BINS] = own[HALF:] + jnp.where(odd == 1, beside, 0.0)
    count = place_ref[1]
    first = jnp.where(count > 0, place_ref[0], 0)
    for slot in range(CAP):
        rows = held[pl.ds(pl.multiple_of((first + slot) * NOFF, 8), NOFF), :]
        rows = jnp.where(slot < count, rows, 0.0)
        real = jnp.zeros((NP, NF), jnp.float32)
        imag = jnp.zeros((NP, NF), jnp.float32)
        for offset in range(NOFF):
            bin_real = rows[offset : offset + 1, :NF]
            bin_imag = rows[offset : offset + 1, NF:]
            cos, sin = slant_ref[0, offset], slant_ref[1, offset]
            real = real + (bin_real * cos + bin_imag * sin)
            imag = imag + (bin_imag * cos - bin_real * sin)
        spec[slot * NP : (slot + 1) * NP, :NF] = real
        spec[slot * NP : (slot + 1) * NP, NF:] = imag
    whole = spec[...]
    high = whole.astype(jnp.bfloat16)
    low = (whole - high.astype(jnp.float32)).astype(jnp.bfloat16)
    traces = jnp.dot(
        jnp.concatenate([high, low, high], axis=1), lags_ref[...], preferred_element_type=jnp.float32
    )
    power = jnp.mean(traces * traces, axis=-1, keepdims=True)
    out_ref[...] = traces / jnp.sqrt(power + 1e-06)


def shards(raw_strain, bin_ids, owner_map):
    count = lax.axis_size("chan")
    periods = lax.axis_size("period")
    smem = pl.BlockSpec(memory_space=pltpu.SMEM)
    vmem = pl.BlockSpec(memory_space=pltpu.VMEM)
    packed = call(pack_kernel, jax.ShapeDtypeStruct((count // 2, 16, 128), jnp.bfloat16))(raw_strain[0])
    series = lax.all_to_all(packed.reshape(count, 8, 128), "chan", 0, 0, tiled=True)
    masks, place = call(
        mask_kernel,
        (
            jax.ShapeDtypeStruct((BINS * CH_DEV, 3 * CH_DEV), jnp.bfloat16),
            jax.ShapeDtypeStruct((2,), jnp.int32),
        ),
        flops=2000000000,
        out_specs=(vmem, smem),
    )(bin_ids, owner_map.reshape(2, 128))
    own = call(spectra_kernel, jax.ShapeDtypeStruct((NWIN, CH_DEV, 2 * NF), jnp.bfloat16))(
        series.reshape(NWIN, 128, 128), jnp.asarray(dft_rows(), jnp.bfloat16)
    )
    near = lax.ppermute(own, "chan", [(i, i + 1) for i in range(count - 1)])
    far = lax.ppermute(own, "chan", [(i, i + 2) for i in range(count - 2)])
    part = jax.ShapeDtypeStruct((HALF, 2 * NF), jnp.float32)
    inside = call(functools.partial(bin_kernel, False), part)(masks, own, near, far)
    pairs = [(i, i + 1) for i in range(0, count, 2)]
    arrived = lax.ppermute(inside, "chan", pairs + [(j, i) for i, j in pairs])
    across = call(functools.partial(bin_kernel, True), part, flops=2000000000)(masks, own, near, far)
    merged = call(merge_kernel, jax.ShapeDtypeStruct((8, BINS, 2 * NF), jnp.bfloat16))(
        across, inside, arrived
    )
    groups = [
        [at % count * periods + p for at in (i + 1, i + 2) for p in range(periods)]
        for i in range(0, count, 2)
    ]
    sums = lax.all_to_all(
        merged, ("chan", "period"), 0, 0, tiled=True, axis_index_groups=groups
    )
    stacks = call(
        stack_kernel,
        jax.ShapeDtypeStruct((CAP * NP, WIN), jnp.float32),
        in_specs=[smem, vmem, vmem, vmem],
        scratch_shapes=[
            pltpu.VMEM((2 * BINS, 2 * NF), jnp.float32),
            pltpu.VMEM((CAP * NP, 2 * NF), jnp.float32),
        ],
    )(place, sums, jnp.asarray(slant_tables()), jnp.asarray(lag_parts()))
    return stacks.reshape(CAP, NP, WIN)


def solution(mesh):
    placed = (P("period", "chan", None), P(None, "chan", None), P())
    return jax.shard_map(
        shards, mesh=mesh, in_specs=placed, out_specs=P("chan", None, None), check_vma=False
    )
```

```python
import functools
import math

import jax
import jax.numpy as jnp
import numpy as np
from jax import lax
from jax.experimental import pallas as pl
from jax.experimental.pallas import tpu as pltpu
from jax.sharding import PartitionSpec as P

CH_DEV = 64
WIN = 256
NF = 128
NWIN = 8
PART = NWIN // 2
MB_DEV = 2
NOFF = 8
NP = 32
CAP = 4
BINS = 2 * MB_DEV * NOFF
HALF = BINS // 2
VMEM_LIMIT = 48 * 1024 * 1024

def dft_rows():
    phase = 2.0 * math.pi / WIN * np.mod(np.arange(WIN)[:, None] * np.arange(1, NF + 1)[None, :], WIN)
    return np.concatenate([np.cos(phase), -np.sin(phase)], axis=1).astype(np.float32)


def lag_table():
    phase = 2.0 * math.pi / WIN * np.mod(np.arange(1, NF + 1)[:, None] * np.arange(WIN)[None, :], WIN)
    return np.concatenate([np.cos(phase), -np.sin(phase)], axis=0).astype(np.float32)


def lag_parts():
    table = lag_table()
    high = table.astype(jnp.bfloat16)
    low = (table - high.astype(np.float32)).astype(jnp.bfloat16)
    return np.concatenate([high, high, low], axis=0)


def slant_tables():
    slow = (np.arange(NP) - NP // 2) / (4.0 * NP)
    offset = (np.arange(NOFF) + 0.5) * (3.0 * CH_DEV / NOFF)
    freq = np.arange(1, NF + 1) * (2.0 * math.pi / WIN)
    phase = offset[:, None, None] * slow[None, :, None] * freq[None, None, :]
    return np.stack([np.cos(phase), np.sin(phase)]).astype(np.float32)


def call(kernel, out_shape, flops=0, **kw):
    return pl.pallas_call(
        kernel,
        out_shape=out_shape,
        cost_estimate=pl.CostEstimate(flops=flops, bytes_accessed=flops // 256, transcendentals=0),
        compiler_params=pltpu.CompilerParams(vmem_limit_bytes=VMEM_LIMIT),
        **kw,
    )


def pack_kernel(raw_ref, out_ref):
    out_ref[0] = jnp.zeros((16, 128), jnp.bfloat16)
    for chip in range(raw_ref.shape[1] // 128):
        tile = raw_ref[:, 128 * chip : 128 * chip + 128]
        out_ref[2 * chip + 1] = tile
        if 2 * chip + 2 < out_ref.shape[0]:
            out_ref[2 * chip + 2] = tile


def mask_kernel(ids_ref, other_ref, owner_ref, masks_ref, place_ref):
    device = lax.axis_index("chan")
    odd = lax.rem(device, 2) == 1
    own = jnp.concatenate([ids_ref[2], ids_ref[1], ids_ref[0]], axis=1)
    other = jnp.concatenate([other_ref[2], other_ref[1], other_ref[0]], axis=1)
    for block in range(2):
        ids = jnp.where(odd, own, other) if block else jnp.where(odd, other, own)
        for bin_at in range(BINS):
            masks_ref[block, bin_at * CH_DEV : (bin_at + 1) * CH_DEV, :] = (
                (ids == bin_at).astype(jnp.float32).astype(jnp.bfloat16)
            )
    owner = owner_ref[...]
    place_ref[0] = jnp.sum((owner < device).astype(jnp.int32)) - MB_DEV * (device - 1)
    place_ref[1] = jnp.sum((owner == device).astype(jnp.int32))


def spectra_kernel(series_ref, table_ref, keep_ref, give_ref):
    table = table_ref[...]
    odd = lax.rem(lax.axis_index("chan"), 2)
    for out_ref, first in ((give_ref, (1 - odd) * PART), (keep_ref, odd * PART)):
        for window in range(PART):
            series = series_ref[first + window].T
            spectra = jnp.dot(series, table, preferred_element_type=jnp.float32)
            power = jnp.mean(spectra * spectra, axis=-1, keepdims=True)
            out_ref[window] = (spectra / jnp.sqrt(power + 1e-06)).astype(jnp.bfloat16)


def add_bins(masks_ref, spectra_ref, sources):
    totals = None
    for block, half in sources:
        rows = slice(half * HALF * CH_DEV, (half + 1) * HALF * CH_DEV)
        for window in range(PART):
            partners = spectra_ref[window, block * CH_DEV : (block + 3) * CH_DEV]
            own = spectra_ref[window, (block + 2) * CH_DEV : (block + 3) * CH_DEV]
            own = own.astype(jnp.float32)
            own_real, own_imag = own[:, :NF], own[:, NF:]
            picked = jnp.dot(masks_ref[block, rows, :], partners, preferred_element_type=jnp.float32)
            terms = []
            for bin_at in range(HALF):
                picked_real = picked[bin_at * CH_DEV : (bin_at + 1) * CH_DEV, :NF]
                picked_imag = picked[bin_at * CH_DEV : (bin_at + 1) * CH_DEV, NF:]
                real = own_real * picked_real + own_imag * picked_imag
                imag = own_imag * picked_real - own_real * picked_imag
                terms.append(jnp.sum(real.reshape(8, 8, NF), axis=0))
                terms.append(jnp.sum(imag.reshape(8, 8, NF), axis=0))
            totals = terms if totals is None else [x + y for x, y in zip(totals, terms)]
    sums = [jnp.sum(total, axis=0, keepdims=True) for total in totals]
    return [jnp.concatenate(sums[2 * k : 2 * k + 2], axis=1) for k in range(HALF)]


def give_kernel(masks_ref, kept_ref, came_ref, spectra_ref, whole_ref):
    odd = lax.rem(lax.axis_index("chan"), 2) == 1
    for window in range(PART):
        kept, came = kept_ref[window], came_ref[window]
        spectra_ref[window, : 2 * CH_DEV] = jnp.where(odd, came, kept)
        spectra_ref[window, 2 * CH_DEV :] = jnp.where(odd, kept, came)
    for bin_at, row in enumerate(add_bins(masks_ref, spectra_ref, ((0, 1), (1, 0)))):
        whole_ref[HALF + bin_at : HALF + bin_at + 1] = row

    @pl.when(odd)
    def _():
        for bin_at, row in enumerate(add_bins(masks_ref, spectra_ref, ((0, 0),))):
            whole_ref[bin_at : bin_at + 1] = row

    @pl.when(jnp.logical_not(odd))
    def _():
        for bin_at, row in enumerate(add_bins(masks_ref, spectra_ref, ((1, 1),))):
            whole_ref[bin_at : bin_at + 1] = row


def keep_kernel(masks_ref, spectra_ref, out_ref):
    odd = lax.rem(lax.axis_index("chan"), 2) == 1

    @pl.when(odd)
    def _():
        for bin_at, row in enumerate(add_bins(masks_ref, spectra_ref, ((1, 1),))):
            out_ref[bin_at : bin_at + 1] = row

    @pl.when(jnp.logical_not(odd))
    def _():
        for bin_at, row in enumerate(add_bins(masks_ref, spectra_ref, ((0, 0),))):
            out_ref[bin_at : bin_at + 1] = row


def merge_kernel(gave_ref, came_ref, edge_ref, out_ref):
    odd = lax.rem(lax.axis_index("chan"), 2) == 1
    edge = (edge_ref[...] + came_ref[:HALF]).astype(jnp.bfloat16)
    middle = (gave_ref[HALF:] + came_ref[HALF:]).astype(jnp.bfloat16)
    merged = jnp.concatenate([jnp.where(odd, middle, edge), jnp.where(odd, edge, middle)], axis=0)
    for place in range(8):
        out_ref[place] = merged


def stack_kernel(place_ref, sums_ref, slant_ref, lags_ref, out_ref, held, spec):
    odd = lax.rem(lax.axis_index("chan"), 2)

    def over_periods(part, rows):
        total = sums_ref[part * 4, rows].astype(jnp.float32)
        for period in range(1, 4):
            total = total + sums_ref[part * 4 + period, rows].astype(jnp.float32)
        return total

    device = lax.axis_index("chan")
    own = over_periods(1 - odd, pl.ds(0, BINS))
    beside = over_periods(odd, pl.ds(pl.multiple_of((1 - odd) * HALF, HALF), HALF))
    beside = jnp.where((device > 0) & (device < lax.axis_size("chan") - 1), beside, 0.0)
    held[...] = jnp.zeros_like(held)
    held[:HALF] = own[:HALF] + jnp.where(odd == 1, 0.0, beside)
    held[HALF:BINS] = own[HALF:] + jnp.where(odd == 1, beside, 0.0)
    count = place_ref[1]
    first = jnp.where(count > 0, place_ref[0], 0)
    for slot in range(CAP):
        rows = held[pl.ds(pl.multiple_of((first + slot) * NOFF, 8), NOFF), :]
        rows = jnp.where(slot < count, rows, 0.0)
        real = jnp.zeros((NP, NF), jnp.float32)
        imag = jnp.zeros((NP, NF), jnp.float32)
        for offset in range(NOFF):
            bin_real = rows[offset : offset + 1, :NF]
            bin_imag = rows[offset : offset + 1, NF:]
            cos, sin = slant_ref[0, offset], slant_ref[1, offset]
            real = real + (bin_real * cos + bin_imag * sin)
            imag = imag + (bin_imag * cos - bin_real * sin)
        spec[slot * NP : (slot + 1) * NP, :NF] = real
        spec[slot * NP : (slot + 1) * NP, NF:] = imag
    whole = spec[...]
    high = whole.astype(jnp.bfloat16)
    low = (whole - high.astype(jnp.float32)).astype(jnp.bfloat16)
    traces = jnp.dot(
        jnp.concatenate([high, low, high], axis=1), lags_ref[...], preferred_element_type=jnp.float32
    )
    power = jnp.mean(traces * traces, axis=-1, keepdims=True)
    out_ref[...] = traces / jnp.sqrt(power + 1e-06)


def shards(raw_strain, bin_ids, owner_map):
    count = lax.axis_size("chan")
    periods = lax.axis_size("period")
    smem = pl.BlockSpec(memory_space=pltpu.SMEM)
    vmem = pl.BlockSpec(memory_space=pltpu.VMEM)
    partners = [(i, i + 1) for i in range(0, count, 2)]
    partners = partners + [(j, i) for i, j in partners]
    packed = call(pack_kernel, jax.ShapeDtypeStruct((count, 16, 128), jnp.bfloat16))(raw_strain[0])
    packed, bin_ids, owner_map = lax.optimization_barrier((packed, bin_ids, owner_map))
    series = lax.all_to_all(packed, "chan", 0, 0, tiled=True)
    masks, place = call(
        mask_kernel,
        (
            jax.ShapeDtypeStruct((2, BINS * CH_DEV, 3 * CH_DEV), jnp.bfloat16),
            jax.ShapeDtypeStruct((2,), jnp.int32),
        ),
        flops=2000000000,
        out_specs=(vmem, smem),
    )(bin_ids, lax.ppermute(bin_ids, "chan", partners), owner_map.reshape(2, 128))
    series, masks, place = lax.optimization_barrier((series, masks, place))
    held = jax.ShapeDtypeStruct((PART, 2 * CH_DEV, 2 * NF), jnp.bfloat16)
    kept, gave = call(spectra_kernel, (held, held))(
        series.reshape(NWIN, WIN, 128), jnp.asarray(dft_rows(), jnp.bfloat16)
    )
    came = lax.ppermute(gave, "chan", partners)
    spectra, gave = call(
        give_kernel,
        (
            jax.ShapeDtypeStruct((PART, 4 * CH_DEV, 2 * NF), jnp.bfloat16),
            jax.ShapeDtypeStruct((BINS, 2 * NF), jnp.float32),
        ),
    )(masks, kept, came)
    came = lax.ppermute(gave, "chan", partners)
    edge = call(keep_kernel, jax.ShapeDtypeStruct((HALF, 2 * NF), jnp.float32), flops=1000000000)(
        masks, spectra
    )
    merged = call(merge_kernel, jax.ShapeDtypeStruct((8, BINS, 2 * NF), jnp.bfloat16))(gave, came, edge)
    groups = [
        [at % count * periods + p for at in (i + 1, i + 2) for p in range(periods)]
        for i in range(0, count, 2)
    ]
    sums = lax.all_to_all(
        merged, ("chan", "period"), 0, 0, tiled=True, axis_index_groups=groups
    )
    stacks = call(
        stack_kernel,
        jax.ShapeDtypeStruct((CAP * NP, WIN), jnp.float32),
        in_specs=[smem, vmem, vmem, vmem],
        scratch_shapes=[
            pltpu.VMEM((2 * BINS, 2 * NF), jnp.float32),
            pltpu.VMEM((CAP * NP, 2 * NF), jnp.float32),
        ],
    )(place, sums, jnp.asarray(slant_tables()), jnp.asarray(lag_parts()))
    return stacks.reshape(CAP, NP, WIN)


def solution(mesh):
    placed = (P("period", "chan", None), P(None, "chan", None), P())
    return jax.shard_map(
        shards, mesh=mesh, in_specs=placed, out_specs=P("chan", None, None), check_vma=False
    )
```

```python
import functools
import math

import jax
import jax.numpy as jnp
import numpy as np
from jax import lax
from jax.experimental import pallas as pl
from jax.experimental.pallas import tpu as pltpu
from jax.sharding import PartitionSpec as P

CH_DEV = 64
WIN = 256
NF = 128
NWIN = 8
MB_DEV = 2
NOFF = 8
NP = 32
CAP = 4
BINS = 2 * MB_DEV * NOFF
HALF = BINS // 2
VMEM_LIMIT = 48 * 1024 * 1024

def dft_rows():
    phase = 2.0 * math.pi / WIN * np.mod(np.arange(WIN)[:, None] * np.arange(1, NF + 1)[None, :], WIN)
    return np.concatenate([np.cos(phase), -np.sin(phase)], axis=1).astype(np.float32)


def lag_table():
    phase = 2.0 * math.pi / WIN * np.mod(np.arange(1, NF + 1)[:, None] * np.arange(WIN)[None, :], WIN)
    return np.concatenate([np.cos(phase), -np.sin(phase)], axis=0).astype(np.float32)


def lag_parts():
    table = lag_table()
    high = table.astype(jnp.bfloat16)
    low = (table - high.astype(np.float32)).astype(jnp.bfloat16)
    return np.concatenate([high, high, low], axis=0)


def slant_tables():
    slow = (np.arange(NP) - NP // 2) / (4.0 * NP)
    offset = (np.arange(NOFF) + 0.5) * (3.0 * CH_DEV / NOFF)
    freq = np.arange(1, NF + 1) * (2.0 * math.pi / WIN)
    phase = offset[:, None, None] * slow[None, :, None] * freq[None, None, :]
    return np.stack([np.cos(phase), np.sin(phase)]).astype(np.float32)


def call(kernel, out_shape, flops=0, **kw):
    return pl.pallas_call(
        kernel,
        out_shape=out_shape,
        cost_estimate=pl.CostEstimate(flops=flops, bytes_accessed=flops // 256, transcendentals=0),
        compiler_params=pltpu.CompilerParams(vmem_limit_bytes=VMEM_LIMIT),
        **kw,
    )


def pack_kernel(raw_ref, out_ref):
    out_ref[0] = jnp.zeros((16, 128), jnp.bfloat16)
    for chip in range(raw_ref.shape[1] // 128):
        tile = raw_ref[:, 128 * chip : 128 * chip + 128]
        out_ref[2 * chip + 1] = tile
        if 2 * chip + 2 < out_ref.shape[0]:
            out_ref[2 * chip + 2] = tile


def mask_kernel(ids_ref, owner_ref, masks_ref, place_ref):
    ids = jnp.concatenate([ids_ref[2], ids_ref[1], ids_ref[0]], axis=1)
    for bin_at in range(BINS):
        masks_ref[bin_at * CH_DEV : (bin_at + 1) * CH_DEV, :] = (
            (ids == bin_at).astype(jnp.float32).astype(jnp.bfloat16)
        )
    device = lax.axis_index("chan")
    owner = owner_ref[...]
    place_ref[0] = jnp.sum((owner < device).astype(jnp.int32)) - MB_DEV * (device - 1)
    place_ref[1] = jnp.sum((owner == device).astype(jnp.int32))


def spectra_kernel(series_ref, table_ref, pair_ref, give_ref):
    table = table_ref[...]
    odd = lax.rem(lax.axis_index("chan"), 2) == 1
    for window in range(NWIN):
        spectra = jnp.dot(series_ref[window].T, table, preferred_element_type=jnp.float32)
        power = jnp.mean(spectra * spectra, axis=-1, keepdims=True)
        whitened = (spectra / jnp.sqrt(power + 1e-06)).astype(jnp.bfloat16)
        pair_ref[window] = whitened
        give_ref[window] = jnp.where(odd, whitened[:CH_DEV], whitened[CH_DEV:])


def bin_kernel(across, masks_ref, pair_ref, came_ref, out_ref):
    odd = lax.rem(lax.axis_index("chan"), 2)
    part = odd if across else 1 - odd
    rows = pl.ds(pl.multiple_of(part * HALF * CH_DEV, HALF * CH_DEV), HALF * CH_DEV)
    totals = None
    for window in range(NWIN):
        low, high, came = pair_ref[window, :CH_DEV], pair_ref[window, CH_DEV:], came_ref[window]
        own = jnp.where(odd == 1, high, came)
        partners = jnp.concatenate(
            [jnp.where(odd == 1, came, low), jnp.where(odd == 1, low, high), own], axis=0
        )
        own = own.astype(jnp.float32)
        own_real, own_imag = own[:, :NF], own[:, NF:]
        picked = jnp.dot(masks_ref[rows, :], partners, preferred_element_type=jnp.float32)
        terms = []
        for bin_at in range(HALF):
            picked_real = picked[bin_at * CH_DEV : (bin_at + 1) * CH_DEV, :NF]
            picked_imag = picked[bin_at * CH_DEV : (bin_at + 1) * CH_DEV, NF:]
            real = own_real * picked_real + own_imag * picked_imag
            imag = own_imag * picked_real - own_real * picked_imag
            terms.append(jnp.sum(real.reshape(8, 8, NF), axis=0))
            terms.append(jnp.sum(imag.reshape(8, 8, NF), axis=0))
        totals = terms if totals is None else [x + y for x, y in zip(totals, terms)]
    for bin_at in range(HALF):
        out_ref[bin_at : bin_at + 1, :NF] = jnp.sum(totals[2 * bin_at], axis=0, keepdims=True)
        out_ref[bin_at : bin_at + 1, NF:] = jnp.sum(totals[2 * bin_at + 1], axis=0, keepdims=True)


def merge_kernel(across_ref, inside_ref, arrived_ref, out_ref):
    odd = lax.rem(lax.axis_index("chan"), 2)
    across = (across_ref[...] + arrived_ref[...]).astype(jnp.bfloat16)
    inside = inside_ref[...].astype(jnp.bfloat16)
    merged = jnp.concatenate(
        [jnp.where(odd == 1, inside, across), jnp.where(odd == 1, across, inside)], axis=0
    )
    for place in range(8):
        out_ref[place] = merged


def stack_kernel(place_ref, sums_ref, slant_ref, lags_ref, out_ref, held, spec):
    odd = lax.rem(lax.axis_index("chan"), 2)

    def over_periods(part, rows):
        total = sums_ref[part * 4, rows].astype(jnp.float32)
        for period in range(1, 4):
            total = total + sums_ref[part * 4 + period, rows].astype(jnp.float32)
        return total

    own = over_periods(odd, pl.ds(0, BINS))
    beside = over_periods(1 - odd, pl.ds(pl.multiple_of(odd * HALF, HALF), HALF))
    held[...] = jnp.zeros_like(held)
    held[:HALF] = own[:HALF] + jnp.where(odd == 1, beside, 0.0)
    held[HALF:BINS] = own[HALF:] + jnp.where(odd == 1, 0.0, beside)
    count = place_ref[1]
    first = jnp.where(count > 0, place_ref[0], 0)
    for slot in range(CAP):
        rows = held[pl.ds(pl.multiple_of((first + slot) * NOFF, 8), NOFF), :]
        rows = jnp.where(slot < count, rows, 0.0)
        real = jnp.zeros((NP, NF), jnp.float32)
        imag = jnp.zeros((NP, NF), jnp.float32)
        for offset in range(NOFF):
            bin_real = rows[offset : offset + 1, :NF]
            bin_imag = rows[offset : offset + 1, NF:]
            cos, sin = slant_ref[0, offset], slant_ref[1, offset]
            real = real + (bin_real * cos + bin_imag * sin)
            imag = imag + (bin_imag * cos - bin_real * sin)
        spec[slot * NP : (slot + 1) * NP, :NF] = real
        spec[slot * NP : (slot + 1) * NP, NF:] = imag
    whole = spec[...]
    high = whole.astype(jnp.bfloat16)
    low = (whole - high.astype(jnp.float32)).astype(jnp.bfloat16)
    traces = jnp.dot(
        jnp.concatenate([high, low, high], axis=1), lags_ref[...], preferred_element_type=jnp.float32
    )
    power = jnp.mean(traces * traces, axis=-1, keepdims=True)
    out_ref[...] = traces / jnp.sqrt(power + 1e-06)


def shards(raw_strain, bin_ids, owner_map):
    count = lax.axis_size("chan")
    periods = lax.axis_size("period")
    smem = pl.BlockSpec(memory_space=pltpu.SMEM)
    vmem = pl.BlockSpec(memory_space=pltpu.VMEM)
    packed = call(pack_kernel, jax.ShapeDtypeStruct((count, 16, 128), jnp.bfloat16))(raw_strain[0])
    series = lax.all_to_all(packed, "chan", 0, 0, tiled=True)
    masks, place = call(
        mask_kernel,
        (
            jax.ShapeDtypeStruct((BINS * CH_DEV, 3 * CH_DEV), jnp.bfloat16),
            jax.ShapeDtypeStruct((2,), jnp.int32),
        ),
        flops=2000000000,
        out_specs=(vmem, smem),
    )(bin_ids, owner_map.reshape(2, 128))
    pair, gave = call(
        spectra_kernel,
        (
            jax.ShapeDtypeStruct((NWIN, 2 * CH_DEV, 2 * NF), jnp.bfloat16),
            jax.ShapeDtypeStruct((NWIN, CH_DEV, 2 * NF), jnp.bfloat16),
        ),
    )(series.reshape(NWIN, WIN, 128), jnp.asarray(dft_rows(), jnp.bfloat16))
    cores = [(i, i + 1) for i in range(0, count, 2)]
    came = lax.ppermute(gave, "chan", cores + [(j, i) for i, j in cores])
    part = jax.ShapeDtypeStruct((HALF, 2 * NF), jnp.float32)
    across = call(functools.partial(bin_kernel, True), part)(masks, pair, came)
    pairs = [(2 * k + 1, 2 * k + 2) for k in range(count // 2 - 1)]
    arrived = lax.ppermute(across, "chan", pairs + [(j, i) for i, j in pairs])
    inside = call(functools.partial(bin_kernel, False), part, flops=2000000000)(masks, pair, came)
    merged = call(merge_kernel, jax.ShapeDtypeStruct((8, BINS, 2 * NF), jnp.bfloat16))(
        across, inside, arrived
    )
    groups = [
        [(2 * k + core) * periods + p for core in range(2) for p in range(periods)]
        for k in range(count // 2)
    ]
    sums = lax.all_to_all(
        merged, ("chan", "period"), 0, 0, tiled=True, axis_index_groups=groups
    )
    stacks = call(
        stack_kernel,
        jax.ShapeDtypeStruct((CAP * NP, WIN), jnp.float32),
        in_specs=[smem, vmem, vmem, vmem],
        scratch_shapes=[
            pltpu.VMEM((2 * BINS, 2 * NF), jnp.float32),
            pltpu.VMEM((CAP * NP, 2 * NF), jnp.float32),
        ],
    )(place, sums, jnp.asarray(slant_tables()), jnp.asarray(lag_parts()))
    return stacks.reshape(CAP, NP, WIN)


def solution(mesh):
    placed = (P("period", "chan", None), P(None, "chan", None), P())
    return jax.shard_map(
        shards, mesh=mesh, in_specs=placed, out_specs=P("chan", None, None), check_vma=False
    )
```

```python
import functools
import math

import jax
import jax.numpy as jnp
import numpy as np
from jax import lax
from jax.experimental import pallas as pl
from jax.experimental.pallas import tpu as pltpu
from jax.sharding import PartitionSpec as P

CH_DEV = 64
WIN = 256
NF = 128
NWIN = 8
MB_DEV = 2
NOFF = 8
NP = 32
CAP = 4
BINS = 2 * MB_DEV * NOFF
HALF = BINS // 2
VMEM_LIMIT = 48 * 1024 * 1024

def dft_rows():
    sample = (
        32 * np.arange(8)[None, :, None] + 16 * np.arange(2)[:, None, None] + np.arange(16)[None, None, :]
    ).reshape(2, WIN // 2, 1)
    phase = 2.0 * math.pi / WIN * np.mod(sample * np.arange(1, NF + 1)[None, None, :], WIN)
    return np.concatenate([np.cos(phase), -np.sin(phase)], axis=2).astype(np.float32)


def lag_table():
    phase = 2.0 * math.pi / WIN * np.mod(np.arange(1, NF + 1)[:, None] * np.arange(WIN)[None, :], WIN)
    return np.concatenate([np.cos(phase), -np.sin(phase)], axis=0).astype(np.float32)


def lag_parts():
    table = lag_table()
    high = table.astype(jnp.bfloat16)
    low = (table - high.astype(np.float32)).astype(jnp.bfloat16)
    return np.concatenate([high, high, low], axis=0)


def slant_tables():
    slow = (np.arange(NP) - NP // 2) / (4.0 * NP)
    offset = (np.arange(NOFF) + 0.5) * (3.0 * CH_DEV / NOFF)
    freq = np.arange(1, NF + 1) * (2.0 * math.pi / WIN)
    phase = offset[:, None, None] * slow[None, :, None] * freq[None, None, :]
    return np.stack([np.cos(phase), np.sin(phase)]).astype(np.float32)


def call(kernel, out_shape, flops=0, **kw):
    return pl.pallas_call(
        kernel,
        out_shape=out_shape,
        cost_estimate=pl.CostEstimate(flops=flops, bytes_accessed=flops // 256, transcendentals=0),
        compiler_params=pltpu.CompilerParams(vmem_limit_bytes=VMEM_LIMIT),
        **kw,
    )


def pack_kernel(raw_ref, out_ref):
    out_ref[0, 0] = jnp.zeros((16, 128), jnp.bfloat16)
    for chip in range(out_ref.shape[0]):
        tile = raw_ref[:, 128 * chip : 128 * chip + 128]
        out_ref[chip, 1] = tile
        if chip + 1 < out_ref.shape[0]:
            out_ref[chip + 1, 0] = tile


def mask_kernel(ids_ref, owner_ref, masks_ref, place_ref):
    ids = jnp.concatenate([ids_ref[2], ids_ref[1], ids_ref[0]], axis=1)
    for bin_at in range(BINS):
        masks_ref[bin_at * CH_DEV : (bin_at + 1) * CH_DEV, :] = (
            (ids == bin_at).astype(jnp.float32).astype(jnp.bfloat16)
        )
    device = lax.axis_index("chan")
    owner = owner_ref[...]
    place_ref[0] = jnp.sum((owner < device).astype(jnp.int32)) - MB_DEV * (device - 1)
    place_ref[1] = jnp.sum((owner == device).astype(jnp.int32))


def spectra_kernel(series_ref, came_ref, table_ref, out_ref):
    core = lax.rem(lax.axis_index("chan"), 2)
    odd = core == 1
    table = jnp.concatenate([table_ref[core], table_ref[1 - core]], axis=0)
    for window in range(NWIN):
        turned = []
        for tile in range(2):
            series = series_ref[window, :, tile].reshape(WIN // 2, 128)
            came = came_ref[window, :, tile].reshape(WIN // 2, 128)
            turned.append(jnp.concatenate([series.T, came.T], axis=1))
        low, high = turned
        blocks = jnp.concatenate(
            [
                jnp.where(odd, low[CH_DEV:], low[:CH_DEV]),
                jnp.where(odd, high[:CH_DEV], low[CH_DEV:]),
                jnp.where(odd, high[CH_DEV:], high[:CH_DEV]),
            ],
            axis=0,
        )
        spectra = jnp.dot(blocks, table, preferred_element_type=jnp.float32)
        power = jnp.mean(spectra * spectra, axis=-1, keepdims=True)
        out_ref[window] = (spectra / jnp.sqrt(power + 1e-06)).astype(jnp.bfloat16)


def bin_kernel(across, masks_ref, spectra_ref, out_ref):
    odd = lax.rem(lax.axis_index("chan"), 2)
    part = odd if across else 1 - odd
    rows = pl.ds(pl.multiple_of(part * HALF * CH_DEV, HALF * CH_DEV), HALF * CH_DEV)
    totals = None
    for window in range(NWIN):
        partners = spectra_ref[window]
        own = spectra_ref[window, 2 * CH_DEV :]
        own = own.astype(jnp.float32)
        own_real, own_imag = own[:, :NF], own[:, NF:]
        picked = jnp.dot(masks_ref[rows, :], partners, preferred_element_type=jnp.float32)
        terms = []
        for bin_at in range(HALF):
            picked_real = picked[bin_at * CH_DEV : (bin_at + 1) * CH_DEV, :NF]
            picked_imag = picked[bin_at * CH_DEV : (bin_at + 1) * CH_DEV, NF:]
            real = own_real * picked_real + own_imag * picked_imag
            imag = own_imag * picked_real - own_real * picked_imag
            terms.append(jnp.sum(real.reshape(8, 8, NF), axis=0))
            terms.append(jnp.sum(imag.reshape(8, 8, NF), axis=0))
        totals = terms if totals is None else [x + y for x, y in zip(totals, terms)]
    for bin_at in range(HALF):
        out_ref[bin_at : bin_at + 1, :NF] = jnp.sum(totals[2 * bin_at], axis=0, keepdims=True)
        out_ref[bin_at : bin_at + 1, NF:] = jnp.sum(totals[2 * bin_at + 1], axis=0, keepdims=True)


def merge_kernel(across_ref, inside_ref, arrived_ref, out_ref):
    odd = lax.rem(lax.axis_index("chan"), 2)
    across = (across_ref[...] + arrived_ref[...]).astype(jnp.bfloat16)
    inside = inside_ref[...].astype(jnp.bfloat16)
    merged = jnp.concatenate(
        [jnp.where(odd == 1, inside, across), jnp.where(odd == 1, across, inside)], axis=0
    )
    for place in range(8):
        out_ref[place] = merged


def stack_kernel(place_ref, sums_ref, slant_ref, lags_ref, out_ref, held, spec):
    odd = lax.rem(lax.axis_index("chan"), 2)

    def over_periods(part, rows):
        total = sums_ref[part * 4, rows].astype(jnp.float32)
        for period in range(1, 4):
            total = total + sums_ref[part * 4 + period, rows].astype(jnp.float32)
        return total

    own = over_periods(odd, pl.ds(0, BINS))
    beside = over_periods(1 - odd, pl.ds(pl.multiple_of(odd * HALF, HALF), HALF))
    held[...] = jnp.zeros_like(held)
    held[:HALF] = own[:HALF] + jnp.where(odd == 1, beside, 0.0)
    held[HALF:BINS] = own[HALF:] + jnp.where(odd == 1, 0.0, beside)
    count = place_ref[1]
    first = jnp.where(count > 0, place_ref[0], 0)
    for slot in range(CAP):
        rows = held[pl.ds(pl.multiple_of((first + slot) * NOFF, 8), NOFF), :]
        rows = jnp.where(slot < count, rows, 0.0)
        real = jnp.zeros((NP, NF), jnp.float32)
        imag = jnp.zeros((NP, NF), jnp.float32)
        for offset in range(NOFF):
            bin_real = rows[offset : offset + 1, :NF]
            bin_imag = rows[offset : offset + 1, NF:]
            cos, sin = slant_ref[0, offset], slant_ref[1, offset]
            real = real + (bin_real * cos + bin_imag * sin)
            imag = imag + (bin_imag * cos - bin_real * sin)
        spec[slot * NP : (slot + 1) * NP, :NF] = real
        spec[slot * NP : (slot + 1) * NP, NF:] = imag
    whole = spec[...]
    high = whole.astype(jnp.bfloat16)
    low = (whole - high.astype(jnp.float32)).astype(jnp.bfloat16)
    traces = jnp.dot(
        jnp.concatenate([high, low, high], axis=1), lags_ref[...], preferred_element_type=jnp.float32
    )
    power = jnp.mean(traces * traces, axis=-1, keepdims=True)
    out_ref[...] = traces / jnp.sqrt(power + 1e-06)


def shards(raw_strain, bin_ids, owner_map):
    count = lax.axis_size("chan")
    periods = lax.axis_size("period")
    smem = pl.BlockSpec(memory_space=pltpu.SMEM)
    vmem = pl.BlockSpec(memory_space=pltpu.VMEM)
    packed = call(pack_kernel, jax.ShapeDtypeStruct((count // 2, 2, 16, 128), jnp.bfloat16))(raw_strain[0])
    groups = [list(range(core, count, 2)) for core in range(2)]
    series = lax.all_to_all(packed, "chan", 0, 0, tiled=True, axis_index_groups=groups)
    cores = [(i, i + 1) for i in range(0, count, 2)]
    came = lax.ppermute(series, "chan", cores + [(j, i) for i, j in cores])
    masks, place = call(
        mask_kernel,
        (
            jax.ShapeDtypeStruct((BINS * CH_DEV, 3 * CH_DEV), jnp.bfloat16),
            jax.ShapeDtypeStruct((2,), jnp.int32),
        ),
        flops=2000000000,
        out_specs=(vmem, smem),
    )(bin_ids, owner_map.reshape(2, 128))
    samples = (NWIN, 8, 2, 16, 128)
    spectra = call(spectra_kernel, jax.ShapeDtypeStruct((NWIN, 3 * CH_DEV, 2 * NF), jnp.bfloat16))(
        series.reshape(samples), came.reshape(samples), jnp.asarray(dft_rows(), jnp.bfloat16)
    )
    part = jax.ShapeDtypeStruct((HALF, 2 * NF), jnp.float32)
    across = call(functools.partial(bin_kernel, True), part)(masks, spectra)
    pairs = [(2 * k + 1, 2 * k + 2) for k in range(count // 2 - 1)]
    arrived = lax.ppermute(across, "chan", pairs + [(j, i) for i, j in pairs])
    inside = call(functools.partial(bin_kernel, False), part, flops=2000000000)(masks, spectra)
    merged = call(merge_kernel, jax.ShapeDtypeStruct((8, BINS, 2 * NF), jnp.bfloat16))(
        across, inside, arrived
    )
    groups = [
        [(2 * k + core) * periods + p for core in range(2) for p in range(periods)]
        for k in range(count // 2)
    ]
    sums = lax.all_to_all(
        merged, ("chan", "period"), 0, 0, tiled=True, axis_index_groups=groups
    )
    stacks = call(
        stack_kernel,
        jax.ShapeDtypeStruct((CAP * NP, WIN), jnp.float32),
        in_specs=[smem, vmem, vmem, vmem],
        scratch_shapes=[
            pltpu.VMEM((2 * BINS, 2 * NF), jnp.float32),
            pltpu.VMEM((CAP * NP, 2 * NF), jnp.float32),
        ],
    )(place, sums, jnp.asarray(slant_tables()), jnp.asarray(lag_parts()))
    return stacks.reshape(CAP, NP, WIN)


def solution(mesh):
    placed = (P("period", "chan", None), P(None, "chan", None), P())
    return jax.shard_map(
        shards, mesh=mesh, in_specs=placed, out_specs=P("chan", None, None), check_vma=False
    )
```

```python
import functools
import math

import jax
import jax.numpy as jnp
import numpy as np
from jax import lax
from jax.experimental import pallas as pl
from jax.experimental.pallas import tpu as pltpu
from jax.sharding import PartitionSpec as P

CH_DEV = 64
WIN = 256
NF = 128
NWIN = 8
MB_DEV = 2
NOFF = 8
NP = 32
CAP = 4
BINS = 2 * MB_DEV * NOFF
HALF = BINS // 2
VMEM_LIMIT = 48 * 1024 * 1024

def dft_rows():
    sample = (
        32 * np.arange(8)[None, :, None] + 16 * np.arange(2)[:, None, None] + np.arange(16)[None, None, :]
    ).reshape(2, WIN // 2, 1)
    phase = 2.0 * math.pi / WIN * np.mod(sample * np.arange(1, NF + 1)[None, None, :], WIN)
    return np.concatenate([np.cos(phase), -np.sin(phase)], axis=2).astype(np.float32)


def lag_table():
    phase = 2.0 * math.pi / WIN * np.mod(np.arange(1, NF + 1)[:, None] * np.arange(WIN)[None, :], WIN)
    return np.concatenate([np.cos(phase), -np.sin(phase)], axis=0).astype(np.float32)


def lag_parts():
    table = lag_table()
    high = table.astype(jnp.bfloat16)
    low = (table - high.astype(np.float32)).astype(jnp.bfloat16)
    return np.concatenate([high, high, low], axis=0)


def slant_tables():
    slow = (np.arange(NP) - NP // 2) / (4.0 * NP)
    offset = (np.arange(NOFF) + 0.5) * (3.0 * CH_DEV / NOFF)
    freq = np.arange(1, NF + 1) * (2.0 * math.pi / WIN)
    phase = offset[:, None, None] * slow[None, :, None] * freq[None, None, :]
    return np.stack([np.cos(phase), np.sin(phase)]).astype(np.float32)


def call(kernel, out_shape, flops=0, **kw):
    return pl.pallas_call(
        kernel,
        out_shape=out_shape,
        cost_estimate=pl.CostEstimate(flops=flops, bytes_accessed=flops // 256, transcendentals=0),
        compiler_params=pltpu.CompilerParams(vmem_limit_bytes=VMEM_LIMIT),
        **kw,
    )


CHIP_ORDER = [8 * (at % 8) + (at // 8 + at % 8) % 8 for at in range(64)]


def pack_kernel(raw_ref, out_ref):
    for place, chip in enumerate(CHIP_ORDER):
        at = 128 * chip
        out_ref[place, 1] = raw_ref[:, at : at + 128]
        if chip:
            out_ref[place, 0] = raw_ref[:, at - 128 : at]
        else:
            out_ref[place, 0] = jnp.zeros((16, 128), jnp.bfloat16)


def mask_kernel(ids_ref, owner_ref, masks_ref, place_ref):
    ids = jnp.concatenate([ids_ref[2], ids_ref[1], ids_ref[0]], axis=1)
    for bin_at in range(BINS):
        masks_ref[bin_at * CH_DEV : (bin_at + 1) * CH_DEV, :] = (
            (ids == bin_at).astype(jnp.float32).astype(jnp.bfloat16)
        )
    device = lax.axis_index("chan")
    owner = owner_ref[...]
    place_ref[0] = jnp.sum((owner < device).astype(jnp.int32)) - MB_DEV * (device - 1)
    place_ref[1] = jnp.sum((owner == device).astype(jnp.int32))


def turned_blocks(series_ref, window):
    odd = lax.rem(lax.axis_index("chan"), 2) == 1
    places = [CHIP_ORDER.index(8 * window + z) for z in range(8)]
    low, high = [
        jnp.concatenate([series_ref[place, tile] for place in places], axis=0).T for tile in range(2)
    ]
    return jnp.concatenate(
        [
            jnp.where(odd, low[CH_DEV:], low[:CH_DEV]),
            jnp.where(odd, high[:CH_DEV], low[CH_DEV:]),
            jnp.where(odd, high[CH_DEV:], high[:CH_DEV]),
        ],
        axis=0,
    )


def own_kernel(series_ref, table_ref, out_ref):
    table = table_ref[lax.rem(lax.axis_index("chan"), 2)]
    for window in range(NWIN):
        blocks = turned_blocks(series_ref, window)
        out_ref[window] = jnp.dot(blocks, table, preferred_element_type=jnp.float32)


def spectra_kernel(own_ref, came_ref, table_ref, out_ref):
    table = table_ref[1 - lax.rem(lax.axis_index("chan"), 2)]
    for window in range(NWIN):
        blocks = turned_blocks(came_ref, window)
        spectra = own_ref[window] + jnp.dot(blocks, table, preferred_element_type=jnp.float32)
        power = jnp.mean(spectra * spectra, axis=-1, keepdims=True)
        out_ref[window] = (spectra * (1.0 / jnp.sqrt(power + 1e-06))).astype(jnp.bfloat16)


def bin_kernel(across, masks_ref, spectra_ref, out_ref):
    odd = lax.rem(lax.axis_index("chan"), 2)
    part = odd if across else 1 - odd
    rows = pl.ds(pl.multiple_of(part * HALF * CH_DEV, HALF * CH_DEV), HALF * CH_DEV)
    totals = None
    for window in range(NWIN):
        partners = spectra_ref[window]
        own = spectra_ref[window, 2 * CH_DEV :]
        own = own.astype(jnp.float32)
        own_real, own_imag = own[:, :NF], own[:, NF:]
        picked = jnp.dot(masks_ref[rows, :], partners, preferred_element_type=jnp.float32)
        terms = []
        for bin_at in range(HALF):
            picked_real = picked[bin_at * CH_DEV : (bin_at + 1) * CH_DEV, :NF]
            picked_imag = picked[bin_at * CH_DEV : (bin_at + 1) * CH_DEV, NF:]
            real = own_real * picked_real + own_imag * picked_imag
            imag = own_imag * picked_real - own_real * picked_imag
            terms.append(jnp.sum(real.reshape(8, 8, NF), axis=0))
            terms.append(jnp.sum(imag.reshape(8, 8, NF), axis=0))
        totals = terms if totals is None else [x + y for x, y in zip(totals, terms)]
    for bin_at in range(HALF):
        out_ref[bin_at : bin_at + 1, :NF] = jnp.sum(totals[2 * bin_at], axis=0, keepdims=True)
        out_ref[bin_at : bin_at + 1, NF:] = jnp.sum(totals[2 * bin_at + 1], axis=0, keepdims=True)


def merge_kernel(across_ref, inside_ref, arrived_ref, out_ref):
    odd = lax.rem(lax.axis_index("chan"), 2)
    across = (across_ref[...] + arrived_ref[...]).astype(jnp.bfloat16)
    inside = inside_ref[...].astype(jnp.bfloat16)
    merged = jnp.concatenate(
        [jnp.where(odd == 1, inside, across), jnp.where(odd == 1, across, inside)], axis=0
    )
    for place in range(8):
        out_ref[place] = merged


def stack_kernel(place_ref, sums_ref, slant_ref, lags_ref, out_ref, held, spec):
    odd = lax.rem(lax.axis_index("chan"), 2)

    def over_periods(part, rows):
        total = sums_ref[part * 4, rows].astype(jnp.float32)
        for period in range(1, 4):
            total = total + sums_ref[part * 4 + period, rows].astype(jnp.float32)
        return total

    own = over_periods(odd, pl.ds(0, BINS))
    beside = over_periods(1 - odd, pl.ds(pl.multiple_of(odd * HALF, HALF), HALF))
    held[...] = jnp.zeros_like(held)
    held[:HALF] = own[:HALF] + jnp.where(odd == 1, beside, 0.0)
    held[HALF:BINS] = own[HALF:] + jnp.where(odd == 1, 0.0, beside)
    count = place_ref[1]
    first = jnp.where(count > 0, place_ref[0], 0)
    for slot in range(CAP):
        rows = held[pl.ds(pl.multiple_of((first + slot) * NOFF, 8), NOFF), :]
        rows = jnp.where(slot < count, rows, 0.0)
        real = jnp.zeros((NP, NF), jnp.float32)
        imag = jnp.zeros((NP, NF), jnp.float32)
        for offset in range(NOFF):
            bin_real = rows[offset : offset + 1, :NF]
            bin_imag = rows[offset : offset + 1, NF:]
            cos, sin = slant_ref[0, offset], slant_ref[1, offset]
            real = real + (bin_real * cos + bin_imag * sin)
            imag = imag + (bin_imag * cos - bin_real * sin)
        spec[slot * NP : (slot + 1) * NP, :NF] = real
        spec[slot * NP : (slot + 1) * NP, NF:] = imag
    whole = spec[...]
    high = whole.astype(jnp.bfloat16)
    low = (whole - high.astype(jnp.float32)).astype(jnp.bfloat16)
    traces = jnp.dot(
        jnp.concatenate([high, low, high], axis=1), lags_ref[...], preferred_element_type=jnp.float32
    )
    power = jnp.mean(traces * traces, axis=-1, keepdims=True)
    out_ref[...] = traces * (1.0 / jnp.sqrt(power + 1e-06))


def shards(raw_strain, bin_ids, owner_map):
    count = lax.axis_size("chan")
    periods = lax.axis_size("period")
    smem = pl.BlockSpec(memory_space=pltpu.SMEM)
    vmem = pl.BlockSpec(memory_space=pltpu.VMEM)
    packed = call(pack_kernel, jax.ShapeDtypeStruct((count // 2, 2, 16, 128), jnp.bfloat16))(raw_strain[0])
    groups = [[2 * chip + core for chip in CHIP_ORDER] for core in range(2)]
    series = lax.all_to_all(packed, "chan", 0, 0, tiled=True, axis_index_groups=groups)
    cores = [(i, i + 1) for i in range(0, count, 2)]
    came = lax.ppermute(series, "chan", cores + [(j, i) for i, j in cores])
    masks, place = call(
        mask_kernel,
        (
            jax.ShapeDtypeStruct((BINS * CH_DEV, 3 * CH_DEV), jnp.bfloat16),
            jax.ShapeDtypeStruct((2,), jnp.int32),
        ),
        flops=2000000000,
        out_specs=(vmem, smem),
    )(bin_ids, owner_map.reshape(2, 128))
    table = jnp.asarray(dft_rows(), jnp.bfloat16)
    own = call(
        own_kernel, jax.ShapeDtypeStruct((NWIN, 3 * CH_DEV, 2 * NF), jnp.float32), flops=2000000000
    )(series, table)
    spectra = call(spectra_kernel, jax.ShapeDtypeStruct((NWIN, 3 * CH_DEV, 2 * NF), jnp.bfloat16))(
        own, came, table
    )
    part = jax.ShapeDtypeStruct((HALF, 2 * NF), jnp.float32)
    across = call(functools.partial(bin_kernel, True), part)(masks, spectra)
    pairs = [(2 * k + 1, 2 * k + 2) for k in range(count // 2 - 1)]
    arrived = lax.ppermute(across, "chan", pairs + [(j, i) for i, j in pairs])
    inside = call(functools.partial(bin_kernel, False), part, flops=2000000000)(masks, spectra)
    merged = call(merge_kernel, jax.ShapeDtypeStruct((8, BINS, 2 * NF), jnp.bfloat16))(
        across, inside, arrived
    )
    groups = [
        [(2 * k + core) * periods + p for core in range(2) for p in range(periods)]
        for k in range(count // 2)
    ]
    sums = lax.all_to_all(
        merged, ("chan", "period"), 0, 0, tiled=True, axis_index_groups=groups
    )
    stacks = call(
        stack_kernel,
        jax.ShapeDtypeStruct((CAP * NP, WIN), jnp.float32),
        in_specs=[smem, vmem, vmem, vmem],
        scratch_shapes=[
            pltpu.VMEM((2 * BINS, 2 * NF), jnp.float32),
            pltpu.VMEM((CAP * NP, 2 * NF), jnp.float32),
        ],
    )(place, sums, jnp.asarray(slant_tables()), jnp.asarray(lag_parts()))
    return stacks.reshape(CAP, NP, WIN)


def solution(mesh):
    placed = (P("period", "chan", None), P(None, "chan", None), P())
    return jax.shard_map(
        shards, mesh=mesh, in_specs=placed, out_specs=P("chan", None, None), check_vma=False
    )
```

```python
import functools
import math

import jax
import jax.numpy as jnp
import numpy as np
from jax import lax
from jax.experimental import pallas as pl
from jax.experimental.pallas import tpu as pltpu
from jax.sharding import PartitionSpec as P

CH_DEV = 64
WIN = 256
NF = 128
NWIN = 8
MB_DEV = 2
NOFF = 8
NP = 32
CAP = 4
BINS = 2 * MB_DEV * NOFF
HALF = BINS // 2
VMEM_LIMIT = 48 * 1024 * 1024

def dft_rows():
    sample = (
        32 * np.arange(8)[None, :, None] + 16 * np.arange(2)[:, None, None] + np.arange(16)[None, None, :]
    ).reshape(2, WIN // 2, 1)
    phase = 2.0 * math.pi / WIN * np.mod(sample * np.arange(1, NF + 1)[None, None, :], WIN)
    return np.concatenate([np.cos(phase), -np.sin(phase)], axis=2).astype(np.float32)


def lag_table():
    phase = 2.0 * math.pi / WIN * np.mod(np.arange(1, NF + 1)[:, None] * np.arange(WIN)[None, :], WIN)
    return np.concatenate([np.cos(phase), -np.sin(phase)], axis=0).astype(np.float32)


def lag_parts():
    table = lag_table()
    high = table.astype(jnp.bfloat16)
    low = (table - high.astype(np.float32)).astype(jnp.bfloat16)
    return np.concatenate([high, high, low], axis=0)


def slant_tables():
    slow = (np.arange(NP) - NP // 2) / (4.0 * NP)
    offset = (np.arange(NOFF) + 0.5) * (3.0 * CH_DEV / NOFF)
    freq = np.arange(1, NF + 1) * (2.0 * math.pi / WIN)
    phase = offset[:, None, None] * slow[None, :, None] * freq[None, None, :]
    return np.stack([np.cos(phase), np.sin(phase)]).astype(np.float32)


def call(kernel, out_shape, flops=0, **kw):
    return pl.pallas_call(
        kernel,
        out_shape=out_shape,
        cost_estimate=pl.CostEstimate(flops=flops, bytes_accessed=flops // 256, transcendentals=0),
        compiler_params=pltpu.CompilerParams(vmem_limit_bytes=VMEM_LIMIT),
        **kw,
    )


CHIP_ORDERS = (
    [8 * (at % 8) + (at // 8 + at % 8) % 8 for at in range(64)],
    [8 * (at % 8) + (7 - at // 8 + at % 8) % 8 for at in range(64)],
)


def place_of(chip, odd):
    even_place, odd_place = CHIP_ORDERS[0].index(chip), CHIP_ORDERS[1].index(chip)
    return jnp.where(odd, odd_place, even_place)


def pack_kernel(raw_ref, out_ref):
    odd = lax.rem(lax.axis_index("chan"), 2) == 1
    for chip in range(out_ref.shape[0]):
        place, at = place_of(chip, odd), 128 * chip
        out_ref[place, 1] = raw_ref[:, at : at + 128]
        if chip:
            out_ref[place, 0] = raw_ref[:, at - 128 : at]
        else:
            out_ref[place, 0] = jnp.zeros((16, 128), jnp.bfloat16)


def mask_kernel(ids_ref, owner_ref, masks_ref, place_ref):
    ids = jnp.concatenate([ids_ref[2], ids_ref[1], ids_ref[0]], axis=1)
    for bin_at in range(BINS):
        masks_ref[bin_at * CH_DEV : (bin_at + 1) * CH_DEV, :] = (
            (ids == bin_at).astype(jnp.float32).astype(jnp.bfloat16)
        )
    device = lax.axis_index("chan")
    owner = owner_ref[...]
    place_ref[0] = jnp.sum((owner < device).astype(jnp.int32)) - MB_DEV * (device - 1)
    place_ref[1] = jnp.sum((owner == device).astype(jnp.int32))


def turned_blocks(series_ref, window, came):
    odd = lax.rem(lax.axis_index("chan"), 2) == 1
    listed = jnp.logical_xor(odd, came)
    places = [place_of(8 * window + z, listed) for z in range(8)]
    low, high = [
        jnp.concatenate([series_ref[place, tile] for place in places], axis=0).T for tile in range(2)
    ]
    return jnp.concatenate(
        [
            jnp.where(odd, low[CH_DEV:], low[:CH_DEV]),
            jnp.where(odd, high[:CH_DEV], low[CH_DEV:]),
            jnp.where(odd, high[CH_DEV:], high[:CH_DEV]),
        ],
        axis=0,
    )


def own_kernel(series_ref, table_ref, out_ref):
    table = table_ref[lax.rem(lax.axis_index("chan"), 2)]
    for window in range(NWIN):
        blocks = turned_blocks(series_ref, window, False)
        out_ref[window] = jnp.dot(blocks, table, preferred_element_type=jnp.float32)


def spectra_kernel(own_ref, came_ref, table_ref, out_ref):
    table = table_ref[1 - lax.rem(lax.axis_index("chan"), 2)]
    for window in range(NWIN):
        blocks = turned_blocks(came_ref, window, True)
        spectra = own_ref[window] + jnp.dot(blocks, table, preferred_element_type=jnp.float32)
        power = jnp.mean(spectra * spectra, axis=-1, keepdims=True)
        out_ref[window] = (spectra * (1.0 / jnp.sqrt(power + 1e-06))).astype(jnp.bfloat16)


def bin_kernel(across, masks_ref, spectra_ref, out_ref):
    odd = lax.rem(lax.axis_index("chan"), 2)
    part = odd if across else 1 - odd
    rows = pl.ds(pl.multiple_of(part * HALF * CH_DEV, HALF * CH_DEV), HALF * CH_DEV)
    totals = None
    for window in range(NWIN):
        partners = spectra_ref[window]
        own = spectra_ref[window, 2 * CH_DEV :]
        own = own.astype(jnp.float32)
        own_real, own_imag = own[:, :NF], own[:, NF:]
        picked = jnp.dot(masks_ref[rows, :], partners, preferred_element_type=jnp.float32)
        terms = []
        for bin_at in range(HALF):
            picked_real = picked[bin_at * CH_DEV : (bin_at + 1) * CH_DEV, :NF]
            picked_imag = picked[bin_at * CH_DEV : (bin_at + 1) * CH_DEV, NF:]
            real = own_real * picked_real + own_imag * picked_imag
            imag = own_imag * picked_real - own_real * picked_imag
            terms.append(jnp.sum(real.reshape(8, 8, NF), axis=0))
            terms.append(jnp.sum(imag.reshape(8, 8, NF), axis=0))
        totals = terms if totals is None else [x + y for x, y in zip(totals, terms)]
    for bin_at in range(HALF):
        out_ref[bin_at : bin_at + 1, :NF] = jnp.sum(totals[2 * bin_at], axis=0, keepdims=True)
        out_ref[bin_at : bin_at + 1, NF:] = jnp.sum(totals[2 * bin_at + 1], axis=0, keepdims=True)


def merge_kernel(across_ref, inside_ref, arrived_ref, out_ref):
    odd = lax.rem(lax.axis_index("chan"), 2)
    across = (across_ref[...] + arrived_ref[...]).astype(jnp.bfloat16)
    inside = inside_ref[...].astype(jnp.bfloat16)
    merged = jnp.concatenate(
        [jnp.where(odd == 1, inside, across), jnp.where(odd == 1, across, inside)], axis=0
    )
    for place in range(8):
        out_ref[place] = merged


def stack_kernel(place_ref, sums_ref, slant_ref, lags_ref, out_ref, held, spec):
    odd = lax.rem(lax.axis_index("chan"), 2)

    def over_periods(part, rows):
        total = sums_ref[part * 4, rows].astype(jnp.float32)
        for period in range(1, 4):
            total = total + sums_ref[part * 4 + period, rows].astype(jnp.float32)
        return total

    own = over_periods(odd, pl.ds(0, BINS))
    beside = over_periods(1 - odd, pl.ds(pl.multiple_of(odd * HALF, HALF), HALF))
    held[...] = jnp.zeros_like(held)
    held[:HALF] = own[:HALF] + jnp.where(odd == 1, beside, 0.0)
    held[HALF:BINS] = own[HALF:] + jnp.where(odd == 1, 0.0, beside)
    count = place_ref[1]
    first = jnp.where(count > 0, place_ref[0], 0)
    for slot in range(CAP):
        rows = held[pl.ds(pl.multiple_of((first + slot) * NOFF, 8), NOFF), :]
        rows = jnp.where(slot < count, rows, 0.0)
        real = jnp.zeros((NP, NF), jnp.float32)
        imag = jnp.zeros((NP, NF), jnp.float32)
        for offset in range(NOFF):
            bin_real = rows[offset : offset + 1, :NF]
            bin_imag = rows[offset : offset + 1, NF:]
            cos, sin = slant_ref[0, offset], slant_ref[1, offset]
            real = real + (bin_real * cos + bin_imag * sin)
            imag = imag + (bin_imag * cos - bin_real * sin)
        spec[slot * NP : (slot + 1) * NP, :NF] = real
        spec[slot * NP : (slot + 1) * NP, NF:] = imag
    whole = spec[...]
    high = whole.astype(jnp.bfloat16)
    low = (whole - high.astype(jnp.float32)).astype(jnp.bfloat16)
    traces = jnp.dot(
        jnp.concatenate([high, low, high], axis=1), lags_ref[...], preferred_element_type=jnp.float32
    )
    power = jnp.mean(traces * traces, axis=-1, keepdims=True)
    out_ref[...] = traces * (1.0 / jnp.sqrt(power + 1e-06))


def shards(raw_strain, bin_ids, owner_map):
    count = lax.axis_size("chan")
    periods = lax.axis_size("period")
    smem = pl.BlockSpec(memory_space=pltpu.SMEM)
    vmem = pl.BlockSpec(memory_space=pltpu.VMEM)
    packed = call(pack_kernel, jax.ShapeDtypeStruct((count // 2, 2, 16, 128), jnp.bfloat16))(raw_strain[0])
    groups = [[2 * chip + core for chip in CHIP_ORDERS[core]] for core in range(2)]
    series = lax.all_to_all(packed, "chan", 0, 0, tiled=True, axis_index_groups=groups)
    cores = [(i, i + 1) for i in range(0, count, 2)]
    came = lax.ppermute(series, "chan", cores + [(j, i) for i, j in cores])
    masks, place = call(
        mask_kernel,
        (
            jax.ShapeDtypeStruct((BINS * CH_DEV, 3 * CH_DEV), jnp.bfloat16),
            jax.ShapeDtypeStruct((2,), jnp.int32),
        ),
        flops=2000000000,
        out_specs=(vmem, smem),
    )(bin_ids, owner_map.reshape(2, 128))
    table = jnp.asarray(dft_rows(), jnp.bfloat16)
    own = call(
        own_kernel, jax.ShapeDtypeStruct((NWIN, 3 * CH_DEV, 2 * NF), jnp.float32), flops=2000000000
    )(series, table)
    spectra = call(spectra_kernel, jax.ShapeDtypeStruct((NWIN, 3 * CH_DEV, 2 * NF), jnp.bfloat16))(
        own, came, table
    )
    part = jax.ShapeDtypeStruct((HALF, 2 * NF), jnp.float32)
    across = call(functools.partial(bin_kernel, True), part)(masks, spectra)
    pairs = [(2 * k + 1, 2 * k + 2) for k in range(count // 2 - 1)]
    arrived = lax.ppermute(across, "chan", pairs + [(j, i) for i, j in pairs])
    inside = call(functools.partial(bin_kernel, False), part, flops=2000000000)(masks, spectra)
    merged = call(merge_kernel, jax.ShapeDtypeStruct((8, BINS, 2 * NF), jnp.bfloat16))(
        across, inside, arrived
    )
    groups = [
        [(2 * k + core) * periods + p for core in range(2) for p in range(periods)]
        for k in range(count // 2)
    ]
    sums = lax.all_to_all(
        merged, ("chan", "period"), 0, 0, tiled=True, axis_index_groups=groups
    )
    stacks = call(
        stack_kernel,
        jax.ShapeDtypeStruct((CAP * NP, WIN), jnp.float32),
        in_specs=[smem, vmem, vmem, vmem],
        scratch_shapes=[
            pltpu.VMEM((2 * BINS, 2 * NF), jnp.float32),
            pltpu.VMEM((CAP * NP, 2 * NF), jnp.float32),
        ],
    )(place, sums, jnp.asarray(slant_tables()), jnp.asarray(lag_parts()))
    return stacks.reshape(CAP, NP, WIN)


def solution(mesh):
    placed = (P("period", "chan", None), P(None, "chan", None), P())
    return jax.shard_map(
        shards, mesh=mesh, in_specs=placed, out_specs=P("chan", None, None), check_vma=False
    )
```

```python
import functools
import math

import jax
import jax.numpy as jnp
import numpy as np
from jax import lax
from jax.experimental import pallas as pl
from jax.experimental.pallas import tpu as pltpu
from jax.sharding import PartitionSpec as P

CH_DEV = 64
WIN = 256
NF = 128
NWIN = 8
MB_DEV = 2
NOFF = 8
NP = 32
CAP = 4
BINS = 2 * MB_DEV * NOFF
HALF = BINS // 2
VMEM_LIMIT = 48 * 1024 * 1024

def dft_rows():
    sample = (
        32 * np.arange(8)[None, :, None] + 16 * np.arange(2)[:, None, None] + np.arange(16)[None, None, :]
    ).reshape(2, WIN // 2, 1)
    phase = 2.0 * math.pi / WIN * np.mod(sample * np.arange(1, NF + 1)[None, None, :], WIN)
    return np.concatenate([np.cos(phase), -np.sin(phase)], axis=2).astype(np.float32)


def lag_table():
    phase = 2.0 * math.pi / WIN * np.mod(np.arange(1, NF + 1)[:, None] * np.arange(WIN)[None, :], WIN)
    return np.concatenate([np.cos(phase), -np.sin(phase)], axis=0).astype(np.float32)


def lag_parts():
    table = lag_table()
    high = table.astype(jnp.bfloat16)
    low = (table - high.astype(np.float32)).astype(jnp.bfloat16)
    return np.concatenate([high, high, low], axis=0)


def slant_tables():
    slow = (np.arange(NP) - NP // 2) / (4.0 * NP)
    offset = (np.arange(NOFF) + 0.5) * (3.0 * CH_DEV / NOFF)
    freq = np.arange(1, NF + 1) * (2.0 * math.pi / WIN)
    phase = offset[:, None, None] * slow[None, :, None] * freq[None, None, :]
    return np.stack([np.cos(phase), np.sin(phase)]).astype(np.float32)


def call(kernel, out_shape, flops=0, **kw):
    return pl.pallas_call(
        kernel,
        out_shape=out_shape,
        cost_estimate=pl.CostEstimate(flops=flops, bytes_accessed=flops // 256, transcendentals=0),
        compiler_params=pltpu.CompilerParams(vmem_limit_bytes=VMEM_LIMIT),
        **kw,
    )


CHIP_ORDERS = (
    [8 * (at % 8) + (at // 8 + at % 8) % 8 for at in range(64)],
    [8 * (7 - at % 8) + (at // 8 + 7 - at % 8) % 8 for at in range(64)],
)


def place_of(chip, odd):
    even_place, odd_place = CHIP_ORDERS[0].index(chip), CHIP_ORDERS[1].index(chip)
    return jnp.where(odd, odd_place, even_place)


def pack_kernel(raw_ref, out_ref):
    odd = lax.rem(lax.axis_index("chan"), 2) == 1
    for chip in range(out_ref.shape[0]):
        place, at = place_of(chip, odd), 128 * chip
        out_ref[place, 1] = raw_ref[:, at : at + 128]
        if chip:
            out_ref[place, 0] = raw_ref[:, at - 128 : at]
        else:
            out_ref[place, 0] = jnp.zeros((16, 128), jnp.bfloat16)


def mask_kernel(ids_ref, owner_ref, masks_ref, place_ref):
    ids = jnp.concatenate([ids_ref[2], ids_ref[1], ids_ref[0]], axis=1)
    for bin_at in range(BINS):
        masks_ref[bin_at * CH_DEV : (bin_at + 1) * CH_DEV, :] = (
            (ids == bin_at).astype(jnp.float32).astype(jnp.bfloat16)
        )
    device = lax.axis_index("chan")
    owner = owner_ref[...]
    place_ref[0] = jnp.sum((owner < device).astype(jnp.int32)) - MB_DEV * (device - 1)
    place_ref[1] = jnp.sum((owner == device).astype(jnp.int32))


def turned_blocks(series_ref, window, came):
    odd = lax.rem(lax.axis_index("chan"), 2) == 1
    listed = jnp.logical_xor(odd, came)
    places = [place_of(8 * window + z, listed) for z in range(8)]
    low, high = [
        jnp.concatenate([series_ref[place, tile] for place in places], axis=0).T for tile in range(2)
    ]
    return jnp.concatenate(
        [
            jnp.where(odd, low[CH_DEV:], low[:CH_DEV]),
            jnp.where(odd, high[:CH_DEV], low[CH_DEV:]),
            jnp.where(odd, high[CH_DEV:], high[:CH_DEV]),
        ],
        axis=0,
    )


def own_kernel(series_ref, table_ref, out_ref):
    table = table_ref[lax.rem(lax.axis_index("chan"), 2)]
    for window in range(NWIN):
        blocks = turned_blocks(series_ref, window, False)
        out_ref[window] = jnp.dot(blocks, table, preferred_element_type=jnp.float32)


def spectra_kernel(own_ref, came_ref, table_ref, out_ref):
    table = table_ref[1 - lax.rem(lax.axis_index("chan"), 2)]
    for window in range(NWIN):
        blocks = turned_blocks(came_ref, window, True)
        spectra = own_ref[window] + jnp.dot(blocks, table, preferred_element_type=jnp.float32)
        power = jnp.mean(spectra * spectra, axis=-1, keepdims=True)
        out_ref[window] = (spectra * (1.0 / jnp.sqrt(power + 1e-06))).astype(jnp.bfloat16)


def bin_kernel(across, masks_ref, spectra_ref, out_ref):
    odd = lax.rem(lax.axis_index("chan"), 2)
    part = odd if across else 1 - odd
    rows = pl.ds(pl.multiple_of(part * HALF * CH_DEV, HALF * CH_DEV), HALF * CH_DEV)
    totals = None
    for window in range(NWIN):
        partners = spectra_ref[window]
        own = spectra_ref[window, 2 * CH_DEV :]
        own = own.astype(jnp.float32)
        own_real, own_imag = own[:, :NF], own[:, NF:]
        picked = jnp.dot(masks_ref[rows, :], partners, preferred_element_type=jnp.float32)
        terms = []
        for bin_at in range(HALF):
            picked_real = picked[bin_at * CH_DEV : (bin_at + 1) * CH_DEV, :NF]
            picked_imag = picked[bin_at * CH_DEV : (bin_at + 1) * CH_DEV, NF:]
            real = own_real * picked_real + own_imag * picked_imag
            imag = own_imag * picked_real - own_real * picked_imag
            terms.append(jnp.sum(real.reshape(8, 8, NF), axis=0))
            terms.append(jnp.sum(imag.reshape(8, 8, NF), axis=0))
        totals = terms if totals is None else [x + y for x, y in zip(totals, terms)]
    for bin_at in range(HALF):
        out_ref[bin_at : bin_at + 1, :NF] = jnp.sum(totals[2 * bin_at], axis=0, keepdims=True)
        out_ref[bin_at : bin_at + 1, NF:] = jnp.sum(totals[2 * bin_at + 1], axis=0, keepdims=True)


def merge_kernel(across_ref, inside_ref, arrived_ref, out_ref):
    odd = lax.rem(lax.axis_index("chan"), 2)
    across = (across_ref[...] + arrived_ref[...]).astype(jnp.bfloat16)
    inside = inside_ref[...].astype(jnp.bfloat16)
    merged = jnp.concatenate(
        [jnp.where(odd == 1, inside, across), jnp.where(odd == 1, across, inside)], axis=0
    )
    for place in range(8):
        out_ref[place] = merged


def stack_kernel(place_ref, sums_ref, slant_ref, lags_ref, out_ref, held, spec):
    odd = lax.rem(lax.axis_index("chan"), 2)

    def over_periods(part, rows):
        total = sums_ref[part * 4, rows].astype(jnp.float32)
        for period in range(1, 4):
            total = total + sums_ref[part * 4 + period, rows].astype(jnp.float32)
        return total

    own = over_periods(odd, pl.ds(0, BINS))
    beside = over_periods(1 - odd, pl.ds(pl.multiple_of(odd * HALF, HALF), HALF))
    held[...] = jnp.zeros_like(held)
    held[:HALF] = own[:HALF] + jnp.where(odd == 1, beside, 0.0)
    held[HALF:BINS] = own[HALF:] + jnp.where(odd == 1, 0.0, beside)
    count = place_ref[1]
    first = jnp.where(count > 0, place_ref[0], 0)
    for slot in range(CAP):
        rows = held[pl.ds(pl.multiple_of((first + slot) * NOFF, 8), NOFF), :]
        rows = jnp.where(slot < count, rows, 0.0)
        real = jnp.zeros((NP, NF), jnp.float32)
        imag = jnp.zeros((NP, NF), jnp.float32)
        for offset in range(NOFF):
            bin_real = rows[offset : offset + 1, :NF]
            bin_imag = rows[offset : offset + 1, NF:]
            cos, sin = slant_ref[0, offset], slant_ref[1, offset]
            real = real + (bin_real * cos + bin_imag * sin)
            imag = imag + (bin_imag * cos - bin_real * sin)
        spec[slot * NP : (slot + 1) * NP, :NF] = real
        spec[slot * NP : (slot + 1) * NP, NF:] = imag
    whole = spec[...]
    high = whole.astype(jnp.bfloat16)
    low = (whole - high.astype(jnp.float32)).astype(jnp.bfloat16)
    traces = jnp.dot(
        jnp.concatenate([high, low, high], axis=1), lags_ref[...], preferred_element_type=jnp.float32
    )
    power = jnp.mean(traces * traces, axis=-1, keepdims=True)
    out_ref[...] = traces * (1.0 / jnp.sqrt(power + 1e-06))


def shards(raw_strain, bin_ids, owner_map):
    count = lax.axis_size("chan")
    periods = lax.axis_size("period")
    smem = pl.BlockSpec(memory_space=pltpu.SMEM)
    vmem = pl.BlockSpec(memory_space=pltpu.VMEM)
    packed = call(pack_kernel, jax.ShapeDtypeStruct((count // 2, 2, 16, 128), jnp.bfloat16))(raw_strain[0])
    groups = [[2 * chip + core for chip in CHIP_ORDERS[core]] for core in range(2)]
    series = lax.all_to_all(packed, "chan", 0, 0, tiled=True, axis_index_groups=groups)
    cores = [(i, i + 1) for i in range(0, count, 2)]
    came = lax.ppermute(series, "chan", cores + [(j, i) for i, j in cores])
    masks, place = call(
        mask_kernel,
        (
            jax.ShapeDtypeStruct((BINS * CH_DEV, 3 * CH_DEV), jnp.bfloat16),
            jax.ShapeDtypeStruct((2,), jnp.int32),
        ),
        flops=2000000000,
        out_specs=(vmem, smem),
    )(bin_ids, owner_map.reshape(2, 128))
    table = jnp.asarray(dft_rows(), jnp.bfloat16)
    own = call(
        own_kernel, jax.ShapeDtypeStruct((NWIN, 3 * CH_DEV, 2 * NF), jnp.float32), flops=2000000000
    )(series, table)
    spectra = call(spectra_kernel, jax.ShapeDtypeStruct((NWIN, 3 * CH_DEV, 2 * NF), jnp.bfloat16))(
        own, came, table
    )
    part = jax.ShapeDtypeStruct((HALF, 2 * NF), jnp.float32)
    across = call(functools.partial(bin_kernel, True), part)(masks, spectra)
    pairs = [(2 * k + 1, 2 * k + 2) for k in range(count // 2 - 1)]
    arrived = lax.ppermute(across, "chan", pairs + [(j, i) for i, j in pairs])
    inside = call(functools.partial(bin_kernel, False), part, flops=2000000000)(masks, spectra)
    merged = call(merge_kernel, jax.ShapeDtypeStruct((8, BINS, 2 * NF), jnp.bfloat16))(
        across, inside, arrived
    )
    groups = [
        [(2 * k + core) * periods + p for core in range(2) for p in range(periods)]
        for k in range(count // 2)
    ]
    sums = lax.all_to_all(
        merged, ("chan", "period"), 0, 0, tiled=True, axis_index_groups=groups
    )
    stacks = call(
        stack_kernel,
        jax.ShapeDtypeStruct((CAP * NP, WIN), jnp.float32),
        in_specs=[smem, vmem, vmem, vmem],
        scratch_shapes=[
            pltpu.VMEM((2 * BINS, 2 * NF), jnp.float32),
            pltpu.VMEM((CAP * NP, 2 * NF), jnp.float32),
        ],
    )(place, sums, jnp.asarray(slant_tables()), jnp.asarray(lag_parts()))
    return stacks.reshape(CAP, NP, WIN)


def solution(mesh):
    placed = (P("period", "chan", None), P(None, "chan", None), P())
    return jax.shard_map(
        shards, mesh=mesh, in_specs=placed, out_specs=P("chan", None, None), check_vma=False
    )
```

```python
import functools
import math

import jax
import jax.numpy as jnp
import numpy as np
from jax import lax
from jax.experimental import pallas as pl
from jax.experimental.pallas import tpu as pltpu
from jax.sharding import PartitionSpec as P

CH_DEV = 64
WIN = 256
NF = 128
NWIN = 8
MB_DEV = 2
NOFF = 8
NP = 32
CAP = 4
BINS = 2 * MB_DEV * NOFF
HALF = BINS // 2
VMEM_LIMIT = 48 * 1024 * 1024

def dft_rows():
    sample = (
        32 * np.arange(8)[None, :, None] + 16 * np.arange(2)[:, None, None] + np.arange(16)[None, None, :]
    ).reshape(2, WIN // 2, 1)
    phase = 2.0 * math.pi / WIN * np.mod(sample * np.arange(1, NF + 1)[None, None, :], WIN)
    return np.concatenate([np.cos(phase), -np.sin(phase)], axis=2).astype(np.float32)


def lag_table():
    phase = 2.0 * math.pi / WIN * np.mod(np.arange(1, NF + 1)[:, None] * np.arange(WIN)[None, :], WIN)
    return np.concatenate([np.cos(phase), -np.sin(phase)], axis=0).astype(np.float32)


def lag_parts():
    table = lag_table()
    high = table.astype(jnp.bfloat16)
    low = (table - high.astype(np.float32)).astype(jnp.bfloat16)
    return np.concatenate([high, high, low], axis=0)


def slant_tables():
    slow = (np.arange(NP) - NP // 2) / (4.0 * NP)
    offset = (np.arange(NOFF) + 0.5) * (3.0 * CH_DEV / NOFF)
    freq = np.arange(1, NF + 1) * (2.0 * math.pi / WIN)
    phase = offset[:, None, None] * slow[None, :, None] * freq[None, None, :]
    return np.stack([np.cos(phase), np.sin(phase)]).astype(np.float32)


def call(kernel, out_shape, flops=0, **kw):
    return pl.pallas_call(
        kernel,
        out_shape=out_shape,
        cost_estimate=pl.CostEstimate(flops=flops, bytes_accessed=flops // 256, transcendentals=0),
        compiler_params=pltpu.CompilerParams(vmem_limit_bytes=VMEM_LIMIT),
        **kw,
    )


CHIP_ORDERS = (
    [8 * (at % 8) + (at // 8 + at % 8) % 8 for at in range(64)],
    [8 * (7 - at % 8) + (at // 8 + at % 8) % 8 for at in range(64)],
)


def place_of(chip, odd):
    even_place, odd_place = CHIP_ORDERS[0].index(chip), CHIP_ORDERS[1].index(chip)
    return jnp.where(odd, odd_place, even_place)


def pack_kernel(raw_ref, out_ref):
    odd = lax.rem(lax.axis_index("chan"), 2) == 1
    for chip in range(out_ref.shape[0]):
        place, at = place_of(chip, odd), 128 * chip
        out_ref[place, 1] = raw_ref[:, at : at + 128]
        if chip:
            out_ref[place, 0] = raw_ref[:, at - 128 : at]
        else:
            out_ref[place, 0] = jnp.zeros((16, 128), jnp.bfloat16)


def mask_kernel(ids_ref, owner_ref, masks_ref, place_ref):
    ids = jnp.concatenate([ids_ref[2], ids_ref[1], ids_ref[0]], axis=1)
    for bin_at in range(BINS):
        masks_ref[bin_at * CH_DEV : (bin_at + 1) * CH_DEV, :] = (
            (ids == bin_at).astype(jnp.float32).astype(jnp.bfloat16)
        )
    device = lax.axis_index("chan")
    owner = owner_ref[...]
    place_ref[0] = jnp.sum((owner < device).astype(jnp.int32)) - MB_DEV * (device - 1)
    place_ref[1] = jnp.sum((owner == device).astype(jnp.int32))


def turned_blocks(series_ref, window, came):
    odd = lax.rem(lax.axis_index("chan"), 2) == 1
    listed = jnp.logical_xor(odd, came)
    places = [place_of(8 * window + z, listed) for z in range(8)]
    low, high = [
        jnp.concatenate([series_ref[place, tile] for place in places], axis=0).T for tile in range(2)
    ]
    return jnp.concatenate(
        [
            jnp.where(odd, low[CH_DEV:], low[:CH_DEV]),
            jnp.where(odd, high[:CH_DEV], low[CH_DEV:]),
            jnp.where(odd, high[CH_DEV:], high[:CH_DEV]),
        ],
        axis=0,
    )


def own_kernel(series_ref, table_ref, out_ref):
    table = table_ref[lax.rem(lax.axis_index("chan"), 2)]
    for window in range(NWIN):
        blocks = turned_blocks(series_ref, window, False)
        out_ref[window] = jnp.dot(blocks, table, preferred_element_type=jnp.float32)


def spectra_kernel(own_ref, came_ref, table_ref, out_ref):
    table = table_ref[1 - lax.rem(lax.axis_index("chan"), 2)]
    for window in range(NWIN):
        blocks = turned_blocks(came_ref, window, True)
        spectra = own_ref[window] + jnp.dot(blocks, table, preferred_element_type=jnp.float32)
        power = jnp.mean(spectra * spectra, axis=-1, keepdims=True)
        out_ref[window] = (spectra * (1.0 / jnp.sqrt(power + 1e-06))).astype(jnp.bfloat16)


def bin_kernel(across, masks_ref, spectra_ref, out_ref):
    odd = lax.rem(lax.axis_index("chan"), 2)
    part = odd if across else 1 - odd
    rows = pl.ds(pl.multiple_of(part * HALF * CH_DEV, HALF * CH_DEV), HALF * CH_DEV)
    totals = None
    for window in range(NWIN):
        partners = spectra_ref[window]
        own = spectra_ref[window, 2 * CH_DEV :]
        own = own.astype(jnp.float32)
        own_real, own_imag = own[:, :NF], own[:, NF:]
        picked = jnp.dot(masks_ref[rows, :], partners, preferred_element_type=jnp.float32)
        terms = []
        for bin_at in range(HALF):
            picked_real = picked[bin_at * CH_DEV : (bin_at + 1) * CH_DEV, :NF]
            picked_imag = picked[bin_at * CH_DEV : (bin_at + 1) * CH_DEV, NF:]
            real = own_real * picked_real + own_imag * picked_imag
            imag = own_imag * picked_real - own_real * picked_imag
            terms.append(jnp.sum(real.reshape(8, 8, NF), axis=0))
            terms.append(jnp.sum(imag.reshape(8, 8, NF), axis=0))
        totals = terms if totals is None else [x + y for x, y in zip(totals, terms)]
    for bin_at in range(HALF):
        out_ref[bin_at : bin_at + 1, :NF] = jnp.sum(totals[2 * bin_at], axis=0, keepdims=True)
        out_ref[bin_at : bin_at + 1, NF:] = jnp.sum(totals[2 * bin_at + 1], axis=0, keepdims=True)


def merge_kernel(across_ref, inside_ref, arrived_ref, out_ref):
    odd = lax.rem(lax.axis_index("chan"), 2)
    across = (across_ref[...] + arrived_ref[...]).astype(jnp.bfloat16)
    inside = inside_ref[...].astype(jnp.bfloat16)
    merged = jnp.concatenate(
        [jnp.where(odd == 1, inside, across), jnp.where(odd == 1, across, inside)], axis=0
    )
    for place in range(8):
        out_ref[place] = merged


def stack_kernel(place_ref, sums_ref, slant_ref, lags_ref, out_ref, held, spec):
    odd = lax.rem(lax.axis_index("chan"), 2)

    def over_periods(part, rows):
        total = sums_ref[part * 4, rows].astype(jnp.float32)
        for period in range(1, 4):
            total = total + sums_ref[part * 4 + period, rows].astype(jnp.float32)
        return total

    own = over_periods(odd, pl.ds(0, BINS))
    beside = over_periods(1 - odd, pl.ds(pl.multiple_of(odd * HALF, HALF), HALF))
    held[...] = jnp.zeros_like(held)
    held[:HALF] = own[:HALF] + jnp.where(odd == 1, beside, 0.0)
    held[HALF:BINS] = own[HALF:] + jnp.where(odd == 1, 0.0, beside)
    count = place_ref[1]
    first = jnp.where(count > 0, place_ref[0], 0)
    for slot in range(CAP):
        rows = held[pl.ds(pl.multiple_of((first + slot) * NOFF, 8), NOFF), :]
        rows = jnp.where(slot < count, rows, 0.0)
        real = jnp.zeros((NP, NF), jnp.float32)
        imag = jnp.zeros((NP, NF), jnp.float32)
        for offset in range(NOFF):
            bin_real = rows[offset : offset + 1, :NF]
            bin_imag = rows[offset : offset + 1, NF:]
            cos, sin = slant_ref[0, offset], slant_ref[1, offset]
            real = real + (bin_real * cos + bin_imag * sin)
            imag = imag + (bin_imag * cos - bin_real * sin)
        spec[slot * NP : (slot + 1) * NP, :NF] = real
        spec[slot * NP : (slot + 1) * NP, NF:] = imag
    whole = spec[...]
    high = whole.astype(jnp.bfloat16)
    low = (whole - high.astype(jnp.float32)).astype(jnp.bfloat16)
    traces = jnp.dot(
        jnp.concatenate([high, low, high], axis=1), lags_ref[...], preferred_element_type=jnp.float32
    )
    power = jnp.mean(traces * traces, axis=-1, keepdims=True)
    out_ref[...] = traces * (1.0 / jnp.sqrt(power + 1e-06))


def shards(raw_strain, bin_ids, owner_map):
    count = lax.axis_size("chan")
    periods = lax.axis_size("period")
    smem = pl.BlockSpec(memory_space=pltpu.SMEM)
    vmem = pl.BlockSpec(memory_space=pltpu.VMEM)
    packed = call(pack_kernel, jax.ShapeDtypeStruct((count // 2, 2, 16, 128), jnp.bfloat16))(raw_strain[0])
    groups = [[2 * chip + core for chip in CHIP_ORDERS[core]] for core in range(2)]
    series = lax.all_to_all(packed, "chan", 0, 0, tiled=True, axis_index_groups=groups)
    cores = [(i, i + 1) for i in range(0, count, 2)]
    came = lax.ppermute(series, "chan", cores + [(j, i) for i, j in cores])
    masks, place = call(
        mask_kernel,
        (
            jax.ShapeDtypeStruct((BINS * CH_DEV, 3 * CH_DEV), jnp.bfloat16),
            jax.ShapeDtypeStruct((2,), jnp.int32),
        ),
        flops=2000000000,
        out_specs=(vmem, smem),
    )(bin_ids, owner_map.reshape(2, 128))
    table = jnp.asarray(dft_rows(), jnp.bfloat16)
    own = call(
        own_kernel, jax.ShapeDtypeStruct((NWIN, 3 * CH_DEV, 2 * NF), jnp.float32), flops=2000000000
    )(series, table)
    spectra = call(spectra_kernel, jax.ShapeDtypeStruct((NWIN, 3 * CH_DEV, 2 * NF), jnp.bfloat16))(
        own, came, table
    )
    part = jax.ShapeDtypeStruct((HALF, 2 * NF), jnp.float32)
    across = call(functools.partial(bin_kernel, True), part)(masks, spectra)
    pairs = [(2 * k + 1, 2 * k + 2) for k in range(count // 2 - 1)]
    arrived = lax.ppermute(across, "chan", pairs + [(j, i) for i, j in pairs])
    inside = call(functools.partial(bin_kernel, False), part, flops=2000000000)(masks, spectra)
    merged = call(merge_kernel, jax.ShapeDtypeStruct((8, BINS, 2 * NF), jnp.bfloat16))(
        across, inside, arrived
    )
    groups = [
        [(2 * k + core) * periods + p for core in range(2) for p in range(periods)]
        for k in range(count // 2)
    ]
    sums = lax.all_to_all(
        merged, ("chan", "period"), 0, 0, tiled=True, axis_index_groups=groups
    )
    stacks = call(
        stack_kernel,
        jax.ShapeDtypeStruct((CAP * NP, WIN), jnp.float32),
        in_specs=[smem, vmem, vmem, vmem],
        scratch_shapes=[
            pltpu.VMEM((2 * BINS, 2 * NF), jnp.float32),
            pltpu.VMEM((CAP * NP, 2 * NF), jnp.float32),
        ],
    )(place, sums, jnp.asarray(slant_tables()), jnp.asarray(lag_parts()))
    return stacks.reshape(CAP, NP, WIN)


def solution(mesh):
    placed = (P("period", "chan", None), P(None, "chan", None), P())
    return jax.shard_map(
        shards, mesh=mesh, in_specs=placed, out_specs=P("chan", None, None), check_vma=False
    )
```
